32 devices in a mesh: section: 2 (over x), dp: 16 (over z, y, core).
Axes of the slice: x: 2, y: 2, z: 4, core: 2. Of those that a mesh axis runs over, the one named last changes fastest.
Arguments:
- activations: bfloat16 [2, 2048, 5120], P('section', 'dp'), may hold values from -200 to 200, as said below
- upstream: bfloat16 [2, 2048, 5120], P('section', 'dp'), may hold values from -120 to 120, as said below
- section_norm_gain: float32 [2, 5120], P('section'), may hold values from 0.1 to 1.9
- adapter_down_weight: bfloat16 [2, 16, 5120], P('section'), may hold values from -0.078125 to 0.078125
- adapter_up_weight: bfloat16 [2, 16, 5120], P('section'), may hold values from -0.078125 to 0.078125
Outputs:
- passed: bfloat16 [2, 2048, 5120], P('section', 'dp')
- grad_pair: bfloat16 [2, 163840], P('section', 'dp')
The draws below stay inside these ranges and needn't reach their ends.
Inputs may be any that keep to these rules, and one draw needn't show every extreme that they name: `activations`: activations of one token position share a part across replicas; rows and features have different scales. `upstream`: gradients of one token position share a part across replicas.
All inputs are finite; a program needn't handle non-finite values.
Results may differ from the reference program's by a relative error of at most 0.0034.
Values may be sent and summed in bfloat16 or wider, within the bound.
A program may use at most 64 MiB of HBM per device.

```python
import math
import jax
import jax.numpy as jnp
from jax import lax

MODEL_WIDTH = 5120
ADAPTER_RANK = 16
TOK_DEV = 128
RELAY_SECTIONS = 2
REPLICAS = 16
ROWS = 2048
LEVELS = 4


def draw_activations(key, part):
    subkeys = jax.random.split(key, 4)
    shared = jnp.clip(jax.random.normal(subkeys[0], (RELAY_SECTIONS, 1, TOK_DEV, MODEL_WIDTH)), -4.0, 4.0)
    private = jnp.clip(jax.random.normal(subkeys[1], (RELAY_SECTIONS, REPLICAS, TOK_DEV, MODEL_WIDTH)), -4.0, 4.0)
    mixture = 0.75 * shared + 0.66 * private
    row_scale = jnp.exp(jax.random.uniform(subkeys[2], (RELAY_SECTIONS, REPLICAS, TOK_DEV, 1), minval=0.0, maxval=math.log(10.0)))
    column_scale = jnp.exp(jax.random.uniform(subkeys[3], (RELAY_SECTIONS, 1, 1, MODEL_WIDTH), minval=0.0, maxval=math.log(10.0)))
    values = mixture * row_scale * column_scale / 3.0
    return values.reshape(RELAY_SECTIONS, ROWS, MODEL_WIDTH).astype(jnp.bfloat16)


def draw_upstream(key, part):
    subkeys = jax.random.split(key, 3)
    shared = jnp.clip(jax.random.normal(subkeys[0], (RELAY_SECTIONS, 1, TOK_DEV, MODEL_WIDTH)), -4.0, 4.0)
    private = jnp.clip(jax.random.normal(subkeys[1], (RELAY_SECTIONS, REPLICAS, TOK_DEV, MODEL_WIDTH)), -4.0, 4.0)
    ramp_scale = 1.0 + 2.0 * jnp.arange(REPLICAS, dtype=jnp.float32).reshape(1, REPLICAS, 1, 1) / (REPLICAS - 1)
    row_scale = jnp.exp(jax.random.uniform(subkeys[2], (RELAY_SECTIONS, REPLICAS, TOK_DEV, 1), minval=0.0, maxval=math.log(2.0)))
    values = (0.75 * shared + 0.66 * private) * ramp_scale * row_scale
    return values.reshape(RELAY_SECTIONS, ROWS, MODEL_WIDTH).astype(jnp.bfloat16)


def levels(stream_key, extent, pieces, smallest, top_value):
    loudness, own = 1.0, jax.random.fold_in(stream_key, 6)
    for dim, parts in pieces:
        heights = jnp.exp(jax.random.uniform(jax.random.fold_in(own, dim), (parts,), jnp.float32, smallest / len(pieces), top_value / len(pieces)))
        loudness = loudness * jnp.repeat(heights, extent[dim] // parts).reshape([-1 if axis == dim else 1 for axis in range(len(extent))])
    return loudness


def scatter_about(key, extent, width, bound, shards=(), held_as=jnp.bfloat16):
    values = width * jax.random.normal(key, extent, jnp.float32)
    if shards:
        values = values * levels(key, extent, shards, -0.22, 0.18)
    return jnp.clip(values, -bound, bound).astype(held_as)


def setup_inputs(seed: int = 0) -> dict:
    key_list = jax.random.split(jax.random.key(seed), 6)
    return {
        "activations": draw_activations(jax.random.fold_in(key_list[5], 71), 0),
        "upstream": draw_upstream(jax.random.fold_in(key_list[5], 71), 0),
        "section_norm_gain": jnp.clip(1.0 + 0.18 * jax.random.normal(key_list[2], (RELAY_SECTIONS, MODEL_WIDTH), jnp.float32), 0.1, 1.9),
        "adapter_down_weight": scatter_about(key_list[3], (RELAY_SECTIONS, ADAPTER_RANK, MODEL_WIDTH), MODEL_WIDTH ** -0.5, 0.078125, ((0, 2),)),
        "adapter_up_weight": scatter_about(key_list[4], (RELAY_SECTIONS, ADAPTER_RANK, MODEL_WIDTH), MODEL_WIDTH ** -0.5, 0.078125, ((0, 2),)),
    }


norm_eps = 1e-05
pair_eps = 1e-06
adapter_scale = 2.0

def replica_backward(inputs, incoming_gradient, gain_row, down_rows, upward_rows):
    widened = inputs.astype(jnp.float32)
    inverse = lax.rsqrt(lax.optimization_barrier(jnp.mean(widened * widened, axis=-1, keepdims=True)) + norm_eps)
    scaled = widened * inverse
    normed = (scaled * gain_row).astype(jnp.bfloat16)
    reduced_gradient = jnp.dot(normed, down_rows.T, preferred_element_type=jnp.float32).astype(jnp.bfloat16)
    count_of_rows = TOK_DEV
    upward_term = adapter_scale * jnp.dot(reduced_gradient.T, incoming_gradient, preferred_element_type=jnp.float32) / count_of_rows
    backward_lowrank = (adapter_scale * jnp.dot(incoming_gradient, upward_rows.T, preferred_element_type=jnp.float32)).astype(jnp.bfloat16)
    down_term = jnp.dot(backward_lowrank.T, normed, preferred_element_type=jnp.float32) / count_of_rows
    back_norm = jnp.dot(backward_lowrank, down_rows, preferred_element_type=jnp.float32) * gain_row
    centre = lax.optimization_barrier(jnp.mean(back_norm * scaled, axis=-1, keepdims=True))
    passed = incoming_gradient.astype(jnp.float32) + inverse * (back_norm - scaled * centre)
    return (passed.astype(jnp.bfloat16), jnp.stack([down_term, upward_term]))

def adasum_levels(vectors):
    for level_bit in range(LEVELS):
        grouped = vectors.reshape(REPLICAS // 2 ** (level_bit + 1), 2, 2 ** level_bit, 2, ADAPTER_RANK * MODEL_WIDTH)
        partner = grouped[:, ::-1].reshape(vectors.shape)
        inner_sum = lax.optimization_barrier(jnp.sum(vectors * partner, axis=-1, keepdims=True))
        own_square = lax.optimization_barrier(jnp.sum(vectors * vectors, axis=-1, keepdims=True))
        far_square = lax.optimization_barrier(jnp.sum(partner * partner, axis=-1, keepdims=True))
        keep_coef = 1.0 - inner_sum / (2.0 * (own_square + pair_eps))
        take_coef = 1.0 - inner_sum / (2.0 * (far_square + pair_eps))
        vectors = keep_coef * vectors + take_coef * partner
    return vectors[0]

def single_section(section_args):
    section_acts, section_grads, gain_row, down_rows, upward_rows = section_args
    section_acts = section_acts.reshape(REPLICAS, TOK_DEV, MODEL_WIDTH)
    section_grads = section_grads.reshape(REPLICAS, TOK_DEV, MODEL_WIDTH)
    passed, gradients = jax.vmap(replica_backward, in_axes=(0, 0, None, None, None))(section_acts, section_grads, gain_row, down_rows, upward_rows)
    merged_gradient = adasum_levels(gradients.reshape(REPLICAS, 2, ADAPTER_RANK * MODEL_WIDTH))
    merged_gradient = merged_gradient.reshape(2 * ADAPTER_RANK * MODEL_WIDTH).astype(jnp.bfloat16)
    return (passed.reshape(ROWS, MODEL_WIDTH), merged_gradient)

def reference(activations, upstream, section_norm_gain, adapter_down_weight, adapter_up_weight):
    passed, merged_gradient = lax.map(single_section, (activations, upstream, section_norm_gain, adapter_down_weight, adapter_up_weight))
    shifted = jnp.concatenate([passed[1:], jnp.zeros_like(passed[:1])], axis=0)
    return (shifted, merged_gradient)
```

```python
import functools

import jax
import jax.numpy as jnp
from jax import lax
from jax.experimental import pallas as pl
from jax.experimental.pallas import tpu as pltpu
from jax.sharding import PartitionSpec as P

norm_eps = 1e-05
pair_eps = 1e-06
adapter_scale = 2.0
LANES = 128
MESH = pl.DeviceIdType.MESH
F32 = jnp.float32
BF16 = jnp.bfloat16

BLOCK_ROWS = (32, 32, 32, 32)
EARLY_BLOCKS = 2
CHUNK = 1024


def contract_last(a, b):
    return lax.dot_general(a, b, (((1,), (1,)), ((), ())), preferred_element_type=F32)


def contract_first(a, b):
    return lax.dot_general(a, b, (((0,), (0,)), ((), ())), preferred_element_type=F32)


def tree_coefficients(gram, n):
    row = lax.broadcasted_iota(jnp.int32, (n, LANES), 0)
    lane = lax.broadcasted_iota(jnp.int32, (n, LANES), 1)
    same = row == lane
    coef = jnp.ones((n, 1), F32)
    step = 1
    while step < n:
        own = jnp.where(same, gram, 0.0)
        cross = jnp.where(lane == (row ^ step), gram, 0.0)

        def factor(axis):
            own_square = jnp.maximum(jnp.sum(own, axis=axis, keepdims=True), 0.0)
            inner = jnp.sum(cross, axis=axis, keepdims=True)
            return 1.0 - inner / (2.0 * (own_square + pair_eps))

        down, across = factor(1), factor(0)
        coef = coef * down
        gram = gram * down * across
        gram = gram + jnp.where(
            (row & step) != 0, pltpu.roll(gram, step, 0), pltpu.roll(gram, n - step, 0)
        )
        gram = gram + jnp.where(
            (lane & step) != 0, pltpu.roll(gram, step, 1), pltpu.roll(gram, LANES - step, 1)
        )
        step *= 2
    return coef


def kernel(
    sections, n, q, pad,
    x_hbm, g_hbm, gain_hbm, down_hbm, up_hbm,
    passed_ref, pair_ref,
    x_ref, g_ref, gain_ref, down_ref, up_ref, normed_ref, grad_ref, zero_ref,
    red_ref, low_ref, inv_ref, cen_ref,
    flat_ref, vsend, vrecv, vwide, gram_send, gram_recv, coef_ref,
    w_sem, x_sem, g_sem, zero_sem,
    pass_send, pass_recv, v_send_sem, v_recv_sem, gram_send_sem, gram_recv_sem,
):
    tokens, width = x_ref.shape
    rank = down_ref.shape[0]
    tiles = width // LANES
    half = n // 2
    section = lax.axis_index("section")
    me = lax.axis_index("dp")
    sends = section > 0
    receives = section < sections - 1
    before = lax.rem(section + sections - 1, sections)

    starts = [sum(BLOCK_ROWS[:b]) for b in range(len(BLOCK_ROWS))]
    blocks = [pl.ds(start, rows) for start, rows in zip(starts, BLOCK_ROWS)]

    weights = [
        pltpu.make_async_copy(up_hbm.at[0], up_ref, w_sem.at[0]),
        pltpu.make_async_copy(down_hbm.at[0], down_ref, w_sem.at[1]),
        pltpu.make_async_copy(gain_hbm, gain_ref, w_sem.at[2]),
    ]
    x_in = [pltpu.make_async_copy(x_hbm.at[0, r], x_ref.at[r], x_sem.at[b]) for b, r in enumerate(blocks)]
    g_in = [pltpu.make_async_copy(g_hbm.at[0, r], g_ref.at[r], g_sem.at[b]) for b, r in enumerate(blocks)]
    x_in[0].start()
    weights[0].start()
    g_in[0].start()
    weights[1].start()
    weights[2].start()
    for b in range(1, len(blocks)):
        x_in[b].start()
        g_in[b].start()

    barrier = pltpu.get_barrier_semaphore()

    def greet(k, carry):
        pl.semaphore_signal(
            barrier, inc=1, device_id=(section, lax.rem(me + k, n)), device_id_type=MESH
        )
        return carry

    @pl.when(sends)
    def _():
        pl.semaphore_signal(barrier, inc=1, device_id=(section - 1, me), device_id_type=MESH)

    @pl.when(receives)
    def _():
        pl.semaphore_signal(barrier, inc=1, device_id=(section + 1, me), device_id_type=MESH)

    lax.fori_loop(1, n, greet, 0)

    def pass_copy(b):
        return pltpu.make_async_remote_copy(
            src_ref=grad_ref.at[blocks[b]],
            dst_ref=passed_ref.at[0, blocks[b]],
            send_sem=pass_send.at[b],
            recv_sem=pass_recv.at[b],
            device_id=(before, me),
            device_id_type=MESH,
        )

    columns = [slice(c, c + CHUNK) for c in range(0, width, CHUNK)]

    def statistics(b):
        rows = slice(starts[b], starts[b] + BLOCK_ROWS[b])
        x_in[b].wait()
        squares = jnp.zeros((BLOCK_ROWS[b], LANES), F32)
        for c in range(0, width, LANES):
            wide = x_ref[rows, c : c + LANES].astype(F32)
            squares = squares + wide * wide
        inverse = lax.rsqrt(jnp.sum(squares, axis=1, keepdims=True) / width + norm_eps)
        g_in[b].wait()
        if b == 0:
            for copy in weights:
                copy.wait()
        low = jnp.zeros((BLOCK_ROWS[b], rank), F32)
        red = jnp.zeros((BLOCK_ROWS[b], rank), F32)
        for c in columns:
            low = low + contract_last(g_ref[rows, c], up_ref[:, c])
            normed = (x_ref[rows, c].astype(F32) * inverse * gain_ref[:, c]).astype(BF16)
            normed_ref[rows, c] = normed
            red = red + contract_last(normed, down_ref[:, c])
        low = (adapter_scale * low).astype(BF16)
        low_ref[rows, :] = low
        red_ref[rows, :] = red.astype(BF16)
        inv_ref[rows, :] = inverse
        cen_ref[rows, :] = jnp.sum(low.astype(F32) * red, axis=1, keepdims=True) / width

    def relay(b):
        rows = slice(starts[b], starts[b] + BLOCK_ROWS[b])

        @pl.when(sends)
        def _():
            inverse = inv_ref[rows, :]
            shift = inverse * cen_ref[rows, :]
            low = low_ref[rows, :]
            for c in columns:
                back = jnp.dot(low, down_ref[:, c], preferred_element_type=F32) * gain_ref[:, c]
                grad = g_ref[rows, c].astype(F32) + inverse * (back - x_ref[rows, c].astype(F32) * shift)
                grad_ref[rows, c] = grad.astype(BF16)
            pass_copy(b).start()

    statistics(0)
    from_sections = jnp.where(sends, 1, 0) + jnp.where(receives, 1, 0)
    pl.semaphore_wait(barrier, n - 1 + from_sections)
    relay(0)

    @pl.when(jnp.logical_not(receives))
    def _():
        zero_ref[...] = jnp.zeros_like(zero_ref)
        for b, r in enumerate(blocks):
            pltpu.make_async_copy(
                zero_ref.at[pl.ds(0, BLOCK_ROWS[b])], passed_ref.at[0, r], zero_sem.at[b]
            ).start()

    for b in range(1, len(blocks)):
        statistics(b)
        if b < EARLY_BLOCKS:
            relay(b)

    if pad != q:
        flat_ref[...] = jnp.zeros_like(flat_ref)
        stride = (tiles // q) * pad
    else:
        stride = tiles
    for c in range(0, width, CHUNK):
        down_term = contract_first(low_ref[...], normed_ref[:, c : c + CHUNK]) / tokens
        up_term = adapter_scale * contract_first(red_ref[...], g_ref[:, c : c + CHUNK]) / tokens
        for t, term in enumerate((down_term, up_term)):
            for inner in range(CHUNK // LANES):
                tile = c // LANES + inner
                place = tile if pad == q else (tile // q) * pad + tile % q
                flat_ref[pl.ds(t * half * pad + place, rank, stride=stride), :] = (
                    term[:, inner * LANES : (inner + 1) * LANES]
                )

    def pack(d, carry):
        vsend[d] = flat_ref[pl.ds(pl.multiple_of(d * pad, 8), pad), :].astype(BF16)
        return carry

    lax.fori_loop(0, n, pack, 0)

    def v_copy(k):
        to = lax.rem(me + k, n)
        return pltpu.make_async_remote_copy(
            src_ref=vsend.at[to],
            dst_ref=vrecv.at[me],
            send_sem=v_send_sem.at[k],
            recv_sem=v_recv_sem.at[k],
            device_id=(section, to),
            device_id_type=MESH,
        )

    def v_arrival(k):
        source = lax.rem(me + n - k, n)
        return pltpu.make_async_remote_copy(
            src_ref=vsend.at[source],
            dst_ref=vrecv.at[source],
            send_sem=v_send_sem.at[k],
            recv_sem=v_recv_sem.at[k],
            device_id=(section, source),
            device_id_type=MESH,
        )

    def v_start(k, carry):
        v_copy(k).start()
        return carry

    lax.fori_loop(1, n, v_start, 0)
    vwide[me] = vsend[me].astype(F32)

    for b in range(EARLY_BLOCKS, len(blocks)):
        relay(b)

    def v_wait(k, carry):
        v_arrival(k).wait_recv()
        source = lax.rem(me + n - k, n)
        vwide[source] = vrecv[source].astype(F32)
        return carry

    lax.fori_loop(1, n, v_wait, 0)

    lane = lax.broadcasted_iota(jnp.int32, (n, LANES), 1)

    def gram_column(i, gram):
        products = jnp.sum(vwide[...] * vwide[i][None], axis=1)
        return jnp.where(lane == i, jnp.sum(products, axis=1, keepdims=True), gram)

    gram_send[...] = lax.fori_loop(0, n, gram_column, jnp.zeros((n, LANES), F32))

    base = (me // half) * half
    place = me - base

    def gram_copy(k):
        to = lax.rem(place + k, half)
        return pltpu.make_async_remote_copy(
            src_ref=gram_send,
            dst_ref=gram_recv.at[place],
            send_sem=gram_send_sem.at[k],
            recv_sem=gram_recv_sem.at[k],
            device_id=(section, base + to),
            device_id_type=MESH,
        )

    def gram_arrival(k):
        source = lax.rem(place + half - k, half)
        return pltpu.make_async_remote_copy(
            src_ref=gram_send,
            dst_ref=gram_recv.at[source],
            send_sem=gram_send_sem.at[k],
            recv_sem=gram_recv_sem.at[k],
            device_id=(section, base + source),
            device_id_type=MESH,
        )

    def gram_start(k, carry):
        gram_copy(k).start()
        return carry

    lax.fori_loop(1, half, gram_start, 0)
    gram_recv[place] = gram_send[...]

    def gram_wait(k, carry):
        gram_arrival(k).wait_recv()
        return carry

    lax.fori_loop(1, half, gram_wait, 0)

    coef = tree_coefficients(jnp.sum(gram_recv[...], axis=0), n)
    coef_ref[...] = jnp.broadcast_to(coef, (n, LANES))

    def weigh(i, total):
        return total + coef_ref[pl.ds(i, 1), :] * vwide[i]

    total = lax.fori_loop(0, n, weigh, jnp.zeros((pad, LANES), F32))
    for tile in range(q):
        pair_ref[:, tile * LANES : (tile + 1) * LANES] = total[tile : tile + 1, :].astype(BF16)

    def sent(k, carry):
        v_copy(k).wait_send()
        return carry

    lax.fori_loop(1, n, sent, 0)

    def gram_sent(k, carry):
        gram_copy(k).wait_send()
        return carry

    lax.fori_loop(1, half, gram_sent, 0)

    @pl.when(jnp.logical_not(receives))
    def _():
        for b, r in enumerate(blocks):
            pltpu.make_async_copy(
                zero_ref.at[pl.ds(0, BLOCK_ROWS[b])], passed_ref.at[0, r], zero_sem.at[b]
            ).wait()

    @pl.when(sends)
    def _():
        for b in range(len(blocks)):
            pass_copy(b).wait_send()

    @pl.when(receives)
    def _():
        for b in range(len(blocks)):
            pass_copy(b).wait_recv()


def per_device(sections, n, activations, upstream, gain, down, up):
    _, tokens, width = activations.shape
    rank = down.shape[1]
    share = 2 * rank * width // n
    q = share // LANES
    pad = q if share >= width else -(-q // 16) * 16
    count = len(BLOCK_ROWS)
    anywhere = pl.BlockSpec(memory_space=pl.ANY)
    return pl.pallas_call(
        functools.partial(kernel, sections, n, q, pad),
        out_shape=(
            jax.ShapeDtypeStruct(activations.shape, BF16),
            jax.ShapeDtypeStruct((1, share), BF16),
        ),
        in_specs=[pl.BlockSpec(memory_space=pltpu.HBM)] * 5,
        out_specs=(anywhere, pl.BlockSpec(memory_space=pltpu.VMEM)),
        scratch_shapes=[
            pltpu.VMEM((tokens, width), BF16),
            pltpu.VMEM((tokens, width), BF16),
            pltpu.VMEM((1, width), F32),
            pltpu.VMEM((rank, width), BF16),
            pltpu.VMEM((rank, width), BF16),
            pltpu.VMEM((tokens, width), BF16),
            pltpu.VMEM((tokens, width), BF16),
            pltpu.VMEM((max(BLOCK_ROWS), width), BF16),
            pltpu.VMEM((tokens, rank), BF16),
            pltpu.VMEM((tokens, rank), BF16),
            pltpu.VMEM((tokens, 1), F32),
            pltpu.VMEM((tokens, 1), F32),
            pltpu.VMEM((n * pad, LANES), F32),
            pltpu.VMEM((n, pad, LANES), BF16),
            pltpu.VMEM((n, pad, LANES), BF16),
            pltpu.VMEM((n, pad, LANES), F32),
            pltpu.VMEM((n, LANES), F32),
            pltpu.VMEM((n // 2, n, LANES), F32),
            pltpu.VMEM((n, LANES), F32),
            pltpu.SemaphoreType.DMA((3,)),
            pltpu.SemaphoreType.DMA((count,)),
            pltpu.SemaphoreType.DMA((count,)),
            pltpu.SemaphoreType.DMA((count,)),
            pltpu.SemaphoreType.DMA((count,)),
            pltpu.SemaphoreType.DMA((count,)),
            pltpu.SemaphoreType.DMA((n,)),
            pltpu.SemaphoreType.DMA((n,)),
            pltpu.SemaphoreType.DMA((n,)),
            pltpu.SemaphoreType.DMA((n,)),
        ],
        compiler_params=pltpu.CompilerParams(
            collective_id=0, has_side_effects=True, vmem_limit_bytes=40 * 2**20
        ),
        cost_estimate=pl.CostEstimate(
            flops=12 * tokens * width * rank, bytes_accessed=6 * tokens * width, transcendentals=0
        ),
    )(activations, upstream, gain, down, up)


def solution(mesh):
    return jax.shard_map(
        functools.partial(per_device, mesh.shape["section"], mesh.shape["dp"]),
        mesh=mesh,
        in_specs=(
            P("section", "dp", None),
            P("section", "dp", None),
            P("section", None),
            P("section", None, None),
            P("section", None, None),
        ),
        out_specs=(P("section", "dp", None), P("section", "dp")),
        check_vma=False,
    )
```

```python
import functools

import jax
import jax.numpy as jnp
from jax import lax
from jax.experimental import pallas as pl
from jax.experimental.pallas import tpu as pltpu
from jax.sharding import PartitionSpec as P

norm_eps = 1e-05
pair_eps = 1e-06
adapter_scale = 2.0
LANES = 128
MESH = pl.DeviceIdType.MESH
F32 = jnp.float32
BF16 = jnp.bfloat16

BLOCK_ROWS = (16, 16, 32, 64)
EARLY_BLOCKS = 3
CHUNK = 1024


def contract_last(a, b):
    return lax.dot_general(a, b, (((1,), (1,)), ((), ())), preferred_element_type=F32)


def contract_first(a, b):
    return lax.dot_general(a, b, (((0,), (0,)), ((), ())), preferred_element_type=F32)


def tree_coefficients(gram, n):
    row = lax.broadcasted_iota(jnp.int32, (n, LANES), 0)
    lane = lax.broadcasted_iota(jnp.int32, (n, LANES), 1)
    same = row == lane
    coef = jnp.ones((n, 1), F32)
    step = 1
    while step < n:
        own = jnp.where(same, gram, 0.0)
        cross = jnp.where(lane == (row ^ step), gram, 0.0)

        def factor(axis):
            own_square = jnp.maximum(jnp.sum(own, axis=axis, keepdims=True), 0.0)
            inner = jnp.sum(cross, axis=axis, keepdims=True)
            return 1.0 - inner / (2.0 * (own_square + pair_eps))

        down, across = factor(1), factor(0)
        coef = coef * down
        gram = gram * down * across
        gram = gram + jnp.where(
            (row & step) != 0, pltpu.roll(gram, step, 0), pltpu.roll(gram, n - step, 0)
        )
        gram = gram + jnp.where(
            (lane & step) != 0, pltpu.roll(gram, step, 1), pltpu.roll(gram, LANES - step, 1)
        )
        step *= 2
    return coef


def kernel(
    sections, n, q, pad,
    x_hbm, g_hbm, gain_hbm, down_hbm, up_hbm,
    passed_ref, pair_ref,
    x_ref, g_ref, gain_ref, down_ref, up_ref, normed_ref, grad_ref, zero_ref,
    red_ref, low_ref, inv_ref, cen_ref,
    flat_ref, vsend, vrecv, vwide, gram_send, gram_recv, coef_ref,
    w_sem, x_sem, g_sem, zero_sem,
    pass_send, pass_recv, v_send_sem, v_recv_sem, gram_send_sem, gram_recv_sem,
):
    tokens, width = x_ref.shape
    rank = down_ref.shape[0]
    tiles = width // LANES
    half = n // 2
    section = lax.axis_index("section")
    me = lax.axis_index("dp")
    sends = section > 0
    receives = section < sections - 1
    before = lax.rem(section + sections - 1, sections)

    starts = [sum(BLOCK_ROWS[:b]) for b in range(len(BLOCK_ROWS))]
    blocks = [pl.ds(start, rows) for start, rows in zip(starts, BLOCK_ROWS)]

    weights = [
        pltpu.make_async_copy(up_hbm.at[0], up_ref, w_sem.at[0]),
        pltpu.make_async_copy(down_hbm.at[0], down_ref, w_sem.at[1]),
        pltpu.make_async_copy(gain_hbm, gain_ref, w_sem.at[2]),
    ]
    x_in = [pltpu.make_async_copy(x_hbm.at[0, r], x_ref.at[r], x_sem.at[b]) for b, r in enumerate(blocks)]
    g_in = [pltpu.make_async_copy(g_hbm.at[0, r], g_ref.at[r], g_sem.at[b]) for b, r in enumerate(blocks)]
    x_in[0].start()
    weights[0].start()
    g_in[0].start()
    weights[1].start()
    weights[2].start()
    for b in range(1, len(blocks)):
        x_in[b].start()
        g_in[b].start()

    barrier = pltpu.get_barrier_semaphore()

    def greet(k, carry):
        pl.semaphore_signal(
            barrier, inc=1, device_id=(section, lax.rem(me + k, n)), device_id_type=MESH
        )
        return carry

    @pl.when(sends)
    def _():
        pl.semaphore_signal(barrier, inc=1, device_id=(section - 1, me), device_id_type=MESH)

    @pl.when(receives)
    def _():
        pl.semaphore_signal(barrier, inc=1, device_id=(section + 1, me), device_id_type=MESH)

    lax.fori_loop(1, n, greet, 0)

    def pass_copy(b):
        return pltpu.make_async_remote_copy(
            src_ref=grad_ref.at[blocks[b]],
            dst_ref=passed_ref.at[0, blocks[b]],
            send_sem=pass_send.at[b],
            recv_sem=pass_recv.at[b],
            device_id=(before, me),
            device_id_type=MESH,
        )

    columns = [slice(c, c + CHUNK) for c in range(0, width, CHUNK)]

    def statistics(b):
        rows = slice(starts[b], starts[b] + BLOCK_ROWS[b])
        x_in[b].wait()
        squares = jnp.zeros((BLOCK_ROWS[b], LANES), F32)
        for c in range(0, width, LANES):
            wide = x_ref[rows, c : c + LANES].astype(F32)
            squares = squares + wide * wide
        inverse = lax.rsqrt(jnp.sum(squares, axis=1, keepdims=True) / width + norm_eps)
        g_in[b].wait()
        if b == 0:
            for copy in weights:
                copy.wait()
        low = jnp.zeros((BLOCK_ROWS[b], rank), F32)
        red = jnp.zeros((BLOCK_ROWS[b], rank), F32)
        for c in columns:
            low = low + contract_last(g_ref[rows, c], up_ref[:, c])
            normed = (x_ref[rows, c].astype(F32) * inverse * gain_ref[:, c]).astype(BF16)
            normed_ref[rows, c] = normed
            red = red + contract_last(normed, down_ref[:, c])
        low = (adapter_scale * low).astype(BF16)
        low_ref[rows, :] = low
        red_ref[rows, :] = red.astype(BF16)
        inv_ref[rows, :] = inverse
        cen_ref[rows, :] = jnp.sum(low.astype(F32) * red, axis=1, keepdims=True) / width

    def relay(b):
        rows = slice(starts[b], starts[b] + BLOCK_ROWS[b])

        @pl.when(sends)
        def _():
            inverse = inv_ref[rows, :]
            shift = inverse * cen_ref[rows, :]
            low = low_ref[rows, :]
            for c in columns:
                back = jnp.dot(low, down_ref[:, c], preferred_element_type=F32) * gain_ref[:, c]
                grad = g_ref[rows, c].astype(F32) + inverse * (back - x_ref[rows, c].astype(F32) * shift)
                grad_ref[rows, c] = grad.astype(BF16)
            pass_copy(b).start()

    statistics(0)
    from_sections = jnp.where(sends, 1, 0) + jnp.where(receives, 1, 0)
    pl.semaphore_wait(barrier, n - 1 + from_sections)
    relay(0)

    @pl.when(jnp.logical_not(receives))
    def _():
        zero_ref[...] = jnp.zeros_like(zero_ref)
        for b, r in enumerate(blocks):
            pltpu.make_async_copy(
                zero_ref.at[pl.ds(0, BLOCK_ROWS[b])], passed_ref.at[0, r], zero_sem.at[b]
            ).start()

    for b in range(1, len(blocks)):
        statistics(b)
        if b < EARLY_BLOCKS:
            relay(b)

    if pad != q:
        flat_ref[...] = jnp.zeros_like(flat_ref)
        stride = (tiles // q) * pad
    else:
        stride = tiles
    for c in range(0, width, CHUNK):
        down_term = contract_first(low_ref[...], normed_ref[:, c : c + CHUNK]) / tokens
        up_term = adapter_scale * contract_first(red_ref[...], g_ref[:, c : c + CHUNK]) / tokens
        for t, term in enumerate((down_term, up_term)):
            for inner in range(CHUNK // LANES):
                tile = c // LANES + inner
                place = tile if pad == q else (tile // q) * pad + tile % q
                flat_ref[pl.ds(t * half * pad + place, rank, stride=stride), :] = (
                    term[:, inner * LANES : (inner + 1) * LANES]
                )

    def pack(d, carry):
        vsend[d] = flat_ref[pl.ds(pl.multiple_of(d * pad, 8), pad), :].astype(BF16)
        return carry

    lax.fori_loop(0, n, pack, 0)

    def v_copy(k):
        to = lax.rem(me + k, n)
        return pltpu.make_async_remote_copy(
            src_ref=vsend.at[to],
            dst_ref=vrecv.at[me],
            send_sem=v_send_sem.at[k],
            recv_sem=v_recv_sem.at[k],
            device_id=(section, to),
            device_id_type=MESH,
        )

    def v_arrival(k):
        source = lax.rem(me + n - k, n)
        return pltpu.make_async_remote_copy(
            src_ref=vsend.at[source],
            dst_ref=vrecv.at[source],
            send_sem=v_send_sem.at[k],
            recv_sem=v_recv_sem.at[k],
            device_id=(section, source),
            device_id_type=MESH,
        )

    def v_start(k, carry):
        v_copy(k).start()
        return carry

    lax.fori_loop(1, n, v_start, 0)
    vwide[me] = vsend[me].astype(F32)

    for b in range(EARLY_BLOCKS, len(blocks)):
        relay(b)

    def v_wait(k, carry):
        v_arrival(k).wait_recv()
        source = lax.rem(me + n - k, n)
        vwide[source] = vrecv[source].astype(F32)
        return carry

    lax.fori_loop(1, n, v_wait, 0)

    lane = lax.broadcasted_iota(jnp.int32, (n, LANES), 1)

    def gram_column(i, gram):
        products = jnp.sum(vwide[...] * vwide[i][None], axis=1)
        return jnp.where(lane == i, jnp.sum(products, axis=1, keepdims=True), gram)

    gram_send[...] = lax.fori_loop(0, n, gram_column, jnp.zeros((n, LANES), F32))

    base = (me // half) * half
    place = me - base

    def gram_copy(k):
        to = lax.rem(place + k, half)
        return pltpu.make_async_remote_copy(
            src_ref=gram_send,
            dst_ref=gram_recv.at[place],
            send_sem=gram_send_sem.at[k],
            recv_sem=gram_recv_sem.at[k],
            device_id=(section, base + to),
            device_id_type=MESH,
        )

    def gram_arrival(k):
        source = lax.rem(place + half - k, half)
        return pltpu.make_async_remote_copy(
            src_ref=gram_send,
            dst_ref=gram_recv.at[source],
            send_sem=gram_send_sem.at[k],
            recv_sem=gram_recv_sem.at[k],
            device_id=(section, base + source),
            device_id_type=MESH,
        )

    def gram_start(k, carry):
        gram_copy(k).start()
        return carry

    lax.fori_loop(1, half, gram_start, 0)
    gram_recv[place] = gram_send[...]

    def gram_wait(k, carry):
        gram_arrival(k).wait_recv()
        return carry

    lax.fori_loop(1, half, gram_wait, 0)

    coef = tree_coefficients(jnp.sum(gram_recv[...], axis=0), n)
    coef_ref[...] = jnp.broadcast_to(coef, (n, LANES))

    def weigh(i, total):
        return total + coef_ref[pl.ds(i, 1), :] * vwide[i]

    total = lax.fori_loop(0, n, weigh, jnp.zeros((pad, LANES), F32))
    for tile in range(q):
        pair_ref[:, tile * LANES : (tile + 1) * LANES] = total[tile : tile + 1, :].astype(BF16)

    def sent(k, carry):
        v_copy(k).wait_send()
        return carry

    lax.fori_loop(1, n, sent, 0)

    def gram_sent(k, carry):
        gram_copy(k).wait_send()
        return carry

    lax.fori_loop(1, half, gram_sent, 0)

    @pl.when(jnp.logical_not(receives))
    def _():
        for b, r in enumerate(blocks):
            pltpu.make_async_copy(
                zero_ref.at[pl.ds(0, BLOCK_ROWS[b])], passed_ref.at[0, r], zero_sem.at[b]
            ).wait()

    @pl.when(sends)
    def _():
        for b in range(len(blocks)):
            pass_copy(b).wait_send()

    @pl.when(receives)
    def _():
        for b in range(len(blocks)):
            pass_copy(b).wait_recv()


def per_device(sections, n, activations, upstream, gain, down, up):
    _, tokens, width = activations.shape
    rank = down.shape[1]
    share = 2 * rank * width // n
    q = share // LANES
    pad = q if share >= width else -(-q // 16) * 16
    count = len(BLOCK_ROWS)
    anywhere = pl.BlockSpec(memory_space=pl.ANY)
    return pl.pallas_call(
        functools.partial(kernel, sections, n, q, pad),
        out_shape=(
            jax.ShapeDtypeStruct(activations.shape, BF16),
            jax.ShapeDtypeStruct((1, share), BF16),
        ),
        in_specs=[pl.BlockSpec(memory_space=pltpu.HBM)] * 5,
        out_specs=(anywhere, pl.BlockSpec(memory_space=pltpu.VMEM)),
        scratch_shapes=[
            pltpu.VMEM((tokens, width), BF16),
            pltpu.VMEM((tokens, width), BF16),
            pltpu.VMEM((1, width), F32),
            pltpu.VMEM((rank, width), BF16),
            pltpu.VMEM((rank, width), BF16),
            pltpu.VMEM((tokens, width), BF16),
            pltpu.VMEM((tokens, width), BF16),
            pltpu.VMEM((max(BLOCK_ROWS), width), BF16),
            pltpu.VMEM((tokens, rank), BF16),
            pltpu.VMEM((tokens, rank), BF16),
            pltpu.VMEM((tokens, 1), F32),
            pltpu.VMEM((tokens, 1), F32),
            pltpu.VMEM((n * pad, LANES), F32),
            pltpu.VMEM((n, pad, LANES), BF16),
            pltpu.VMEM((n, pad, LANES), BF16),
            pltpu.VMEM((n, pad, LANES), F32),
            pltpu.VMEM((n, LANES), F32),
            pltpu.VMEM((n // 2, n, LANES), F32),
            pltpu.VMEM((n, LANES), F32),
            pltpu.SemaphoreType.DMA((3,)),
            pltpu.SemaphoreType.DMA((count,)),
            pltpu.SemaphoreType.DMA((count,)),
            pltpu.SemaphoreType.DMA((count,)),
            pltpu.SemaphoreType.DMA((count,)),
            pltpu.SemaphoreType.DMA((count,)),
            pltpu.SemaphoreType.DMA((n,)),
            pltpu.SemaphoreType.DMA((n,)),
            pltpu.SemaphoreType.DMA((n,)),
            pltpu.SemaphoreType.DMA((n,)),
        ],
        compiler_params=pltpu.CompilerParams(
            collective_id=0, has_side_effects=True, vmem_limit_bytes=40 * 2**20
        ),
        cost_estimate=pl.CostEstimate(
            flops=12 * tokens * width * rank, bytes_accessed=6 * tokens * width, transcendentals=0
        ),
    )(*[pltpu.with_memory_space_constraint(a, pltpu.HBM) for a in (activations, upstream, gain, down, up)])


def solution(mesh):
    return jax.shard_map(
        functools.partial(per_device, mesh.shape["section"], mesh.shape["dp"]),
        mesh=mesh,
        in_specs=(
            P("section", "dp", None),
            P("section", "dp", None),
            P("section", None),
            P("section", None, None),
            P("section", None, None),
        ),
        out_specs=(P("section", "dp", None), P("section", "dp")),
        check_vma=False,
    )
```

```python
import functools

import jax
import jax.numpy as jnp
from jax import lax
from jax.experimental import pallas as pl
from jax.experimental.pallas import tpu as pltpu
from jax.sharding import PartitionSpec as P

norm_eps = 1e-05
pair_eps = 1e-06
adapter_scale = 2.0
LANES = 128
MESH = pl.DeviceIdType.MESH
F32 = jnp.float32
BF16 = jnp.bfloat16

BLOCK_ROWS = (16, 16, 32, 64)
PIECES = 8
CHUNK = 1024


def contract_last(a, b):
    return lax.dot_general(a, b, (((1,), (1,)), ((), ())), preferred_element_type=F32)


def contract_first(a, b):
    return lax.dot_general(a, b, (((0,), (0,)), ((), ())), preferred_element_type=F32)


def tree_coefficients(gram, n):
    row = lax.broadcasted_iota(jnp.int32, (n, LANES), 0)
    lane = lax.broadcasted_iota(jnp.int32, (n, LANES), 1)
    same = row == lane
    coef = jnp.ones((n, 1), F32)
    step = 1
    while step < n:
        own = jnp.where(same, gram, 0.0)
        cross = jnp.where(lane == (row ^ step), gram, 0.0)

        def factor(axis):
            own_square = jnp.maximum(jnp.sum(own, axis=axis, keepdims=True), 0.0)
            inner = jnp.sum(cross, axis=axis, keepdims=True)
            return 1.0 - inner / (2.0 * (own_square + pair_eps))

        down, across = factor(1), factor(0)
        coef = coef * down
        gram = gram * down * across
        gram = gram + jnp.where(
            (row & step) != 0, pltpu.roll(gram, step, 0), pltpu.roll(gram, n - step, 0)
        )
        gram = gram + jnp.where(
            (lane & step) != 0, pltpu.roll(gram, step, 1), pltpu.roll(gram, LANES - step, 1)
        )
        step *= 2
    return coef


def kernel(
    sections, n, q, pad,
    x_hbm, g_hbm, gain_hbm, down_hbm, up_hbm,
    passed_ref, pair_ref,
    x_ref, g_ref, gain_ref, down_ref, up_ref, normed_ref, grad_ref, zero_ref,
    red_ref, low_ref, inv_ref, cen_ref,
    flat_ref, vsend, vrecv, vwide, gram_send, gram_recv, coef_ref,
    w_sem, x_sem, g_sem, zero_sem,
    pass_send, pass_recv, v_send_sem, v_recv_sem, gram_send_sem, gram_recv_sem,
):
    tokens, width = x_ref.shape
    rank = down_ref.shape[0]
    tiles = width // LANES
    half = n // 2
    section = lax.axis_index("section")
    me = lax.axis_index("dp")
    sends = section > 0
    receives = section < sections - 1
    before = lax.rem(section + sections - 1, sections)

    starts = [sum(BLOCK_ROWS[:b]) for b in range(len(BLOCK_ROWS))]
    blocks = [pl.ds(start, rows) for start, rows in zip(starts, BLOCK_ROWS)]

    weights = [
        pltpu.make_async_copy(up_hbm.at[0], up_ref, w_sem.at[0]),
        pltpu.make_async_copy(down_hbm.at[0], down_ref, w_sem.at[1]),
        pltpu.make_async_copy(gain_hbm, gain_ref, w_sem.at[2]),
    ]
    x_in = [pltpu.make_async_copy(x_hbm.at[0, r], x_ref.at[r], x_sem.at[b]) for b, r in enumerate(blocks)]
    g_in = [pltpu.make_async_copy(g_hbm.at[0, r], g_ref.at[r], g_sem.at[b]) for b, r in enumerate(blocks)]
    x_in[0].start()
    weights[0].start()
    g_in[0].start()
    weights[1].start()
    weights[2].start()
    for b in range(1, len(blocks)):
        x_in[b].start()
        g_in[b].start()

    barrier = pltpu.get_barrier_semaphore()

    def greet(k, carry):
        pl.semaphore_signal(
            barrier, inc=1, device_id=(section, lax.rem(me + k, n)), device_id_type=MESH
        )
        return carry

    @pl.when(sends)
    def _():
        pl.semaphore_signal(barrier, inc=1, device_id=(section - 1, me), device_id_type=MESH)

    @pl.when(receives)
    def _():
        pl.semaphore_signal(barrier, inc=1, device_id=(section + 1, me), device_id_type=MESH)

    lax.fori_loop(1, n, greet, 0)

    def pass_copy(b):
        return pltpu.make_async_remote_copy(
            src_ref=grad_ref.at[blocks[b]],
            dst_ref=passed_ref.at[0, blocks[b]],
            send_sem=pass_send.at[b],
            recv_sem=pass_recv.at[b],
            device_id=(before, me),
            device_id_type=MESH,
        )

    columns = [slice(c, c + CHUNK) for c in range(0, width, CHUNK)]

    def statistics(b):
        rows = slice(starts[b], starts[b] + BLOCK_ROWS[b])
        x_in[b].wait()
        squares = jnp.zeros((BLOCK_ROWS[b], LANES), F32)
        for c in range(0, width, LANES):
            wide = x_ref[rows, c : c + LANES].astype(F32)
            squares = squares + wide * wide
        inverse = lax.rsqrt(jnp.sum(squares, axis=1, keepdims=True) / width + norm_eps)
        g_in[b].wait()
        if b == 0:
            for copy in weights:
                copy.wait()
        low = jnp.zeros((BLOCK_ROWS[b], rank), F32)
        red = jnp.zeros((BLOCK_ROWS[b], rank), F32)
        for c in columns:
            low = low + contract_last(g_ref[rows, c], up_ref[:, c])
            normed = (x_ref[rows, c].astype(F32) * inverse * gain_ref[:, c]).astype(BF16)
            normed_ref[rows, c] = normed
            red = red + contract_last(normed, down_ref[:, c])
        low = (adapter_scale * low).astype(BF16)
        low_ref[rows, :] = low
        red_ref[rows, :] = red.astype(BF16)
        inv_ref[rows, :] = inverse
        cen_ref[rows, :] = jnp.sum(low.astype(F32) * red, axis=1, keepdims=True) / width

    def relay(b):
        rows = slice(starts[b], starts[b] + BLOCK_ROWS[b])

        @pl.when(sends)
        def _():
            inverse = inv_ref[rows, :]
            shift = inverse * cen_ref[rows, :]
            low = low_ref[rows, :]
            for c in columns:
                back = jnp.dot(low, down_ref[:, c], preferred_element_type=F32) * gain_ref[:, c]
                grad = g_ref[rows, c].astype(F32) + inverse * (back - x_ref[rows, c].astype(F32) * shift)
                grad_ref[rows, c] = grad.astype(BF16)
            pass_copy(b).start()

    statistics(0)
    from_sections = jnp.where(sends, 1, 0) + jnp.where(receives, 1, 0)
    pl.semaphore_wait(barrier, n - 1 + from_sections)
    relay(0)

    @pl.when(jnp.logical_not(receives))
    def _():
        zero_ref[...] = jnp.zeros_like(zero_ref)
        for b, r in enumerate(blocks):
            pltpu.make_async_copy(
                zero_ref.at[pl.ds(0, BLOCK_ROWS[b])], passed_ref.at[0, r], zero_sem.at[b]
            ).start()

    for b in range(1, len(blocks)):
        statistics(b)
        relay(b)

    if pad != q:
        flat_ref[...] = jnp.zeros_like(flat_ref)
        stride = (tiles // q) * pad
    else:
        stride = tiles
    for c in range(0, width, CHUNK):
        down_term = contract_first(low_ref[...], normed_ref[:, c : c + CHUNK]) / tokens
        up_term = adapter_scale * contract_first(red_ref[...], g_ref[:, c : c + CHUNK]) / tokens
        for t, term in enumerate((down_term, up_term)):
            for inner in range(CHUNK // LANES):
                tile = c // LANES + inner
                place = tile if pad == q else (tile // q) * pad + tile % q
                flat_ref[pl.ds(t * half * pad + place, rank, stride=stride), :] = (
                    term[:, inner * LANES : (inner + 1) * LANES]
                )

    def pack(d, carry):
        vsend[d] = flat_ref[pl.ds(pl.multiple_of(d * pad, 8), pad), :].astype(BF16)
        return carry

    lax.fori_loop(0, n, pack, 0)

    def v_copy(k):
        to = lax.rem(me + k, n)
        return pltpu.make_async_remote_copy(
            src_ref=vsend.at[to],
            dst_ref=vrecv.at[me],
            send_sem=v_send_sem.at[k],
            recv_sem=v_recv_sem.at[k],
            device_id=(section, to),
            device_id_type=MESH,
        )

    def v_arrival(k):
        source = lax.rem(me + n - k, n)
        return pltpu.make_async_remote_copy(
            src_ref=vsend.at[source],
            dst_ref=vrecv.at[source],
            send_sem=v_send_sem.at[k],
            recv_sem=v_recv_sem.at[k],
            device_id=(section, source),
            device_id_type=MESH,
        )

    def v_start(k, carry):
        v_copy(k).start()
        return carry

    lax.fori_loop(1, n, v_start, 0)
    vwide[me] = vsend[me].astype(F32)

    def v_wait(k, carry):
        v_arrival(k).wait_recv()
        source = lax.rem(me + n - k, n)
        vwide[source] = vrecv[source].astype(F32)
        return carry

    lax.fori_loop(1, n, v_wait, 0)

    lane = lax.broadcasted_iota(jnp.int32, (n, LANES), 1)

    def gram_column(i, gram):
        products = jnp.sum(vwide[...] * vwide[i][None], axis=1)
        return jnp.where(lane == i, jnp.sum(products, axis=1, keepdims=True), gram)

    gram_send[...] = lax.fori_loop(0, n, gram_column, jnp.zeros((n, LANES), F32))

    base = (me // half) * half
    place = me - base

    def gram_copy(k):
        to = lax.rem(place + k, half)
        return pltpu.make_async_remote_copy(
            src_ref=gram_send,
            dst_ref=gram_recv.at[place],
            send_sem=gram_send_sem.at[k],
            recv_sem=gram_recv_sem.at[k],
            device_id=(section, base + to),
            device_id_type=MESH,
        )

    def gram_arrival(k):
        source = lax.rem(place + half - k, half)
        return pltpu.make_async_remote_copy(
            src_ref=gram_send,
            dst_ref=gram_recv.at[source],
            send_sem=gram_send_sem.at[k],
            recv_sem=gram_recv_sem.at[k],
            device_id=(section, base + source),
            device_id_type=MESH,
        )

    def gram_start(k, carry):
        gram_copy(k).start()
        return carry

    lax.fori_loop(1, half, gram_start, 0)
    gram_recv[place] = gram_send[...]

    def gram_wait(k, carry):
        gram_arrival(k).wait_recv()
        return carry

    lax.fori_loop(1, half, gram_wait, 0)

    coef = tree_coefficients(jnp.sum(gram_recv[...], axis=0), n)
    coef_ref[...] = jnp.broadcast_to(coef, (n, LANES))

    def weigh(i, total):
        return total + coef_ref[pl.ds(i, 1), :] * vwide[i]

    total = lax.fori_loop(0, n, weigh, jnp.zeros((pad, LANES), F32))
    for tile in range(q):
        pair_ref[:, tile * LANES : (tile + 1) * LANES] = total[tile : tile + 1, :].astype(BF16)

    def sent(k, carry):
        v_copy(k).wait_send()
        return carry

    lax.fori_loop(1, n, sent, 0)

    def gram_sent(k, carry):
        gram_copy(k).wait_send()
        return carry

    lax.fori_loop(1, half, gram_sent, 0)

    @pl.when(jnp.logical_not(receives))
    def _():
        for b, r in enumerate(blocks):
            pltpu.make_async_copy(
                zero_ref.at[pl.ds(0, BLOCK_ROWS[b])], passed_ref.at[0, r], zero_sem.at[b]
            ).wait()

    @pl.when(sends)
    def _():
        for b in range(len(blocks)):
            pass_copy(b).wait_send()

    @pl.when(receives)
    def _():
        for b in range(len(blocks)):
            pass_copy(b).wait_recv()


def store_results(passed_in, pair_in, passed_out, pair_out, sem):
    rows = passed_in.shape[1] // PIECES
    copies = [pltpu.make_async_copy(pair_in, pair_out, sem.at[PIECES])]
    for i in range(PIECES):
        piece = pl.ds(i * rows, rows)
        copies.append(pltpu.make_async_copy(passed_in.at[0, piece], passed_out.at[0, piece], sem.at[i]))
    for copy in copies:
        copy.start()
    for copy in copies:
        copy.wait()


def per_device(sections, n, activations, upstream, gain, down, up):
    _, tokens, width = activations.shape
    rank = down.shape[1]
    share = 2 * rank * width // n
    q = share // LANES
    pad = q if share >= width else -(-q // 16) * 16
    count = len(BLOCK_ROWS)
    anywhere = pl.BlockSpec(memory_space=pl.ANY)
    shapes = (
        jax.ShapeDtypeStruct(activations.shape, BF16),
        jax.ShapeDtypeStruct((1, share), BF16),
    )
    held = pl.pallas_call(
        functools.partial(kernel, sections, n, q, pad),
        out_shape=shapes,
        in_specs=[pl.BlockSpec(memory_space=pltpu.HBM)] * 5,
        out_specs=(anywhere, pl.BlockSpec(memory_space=pltpu.VMEM)),
        scratch_shapes=[
            pltpu.VMEM((tokens, width), BF16),
            pltpu.VMEM((tokens, width), BF16),
            pltpu.VMEM((1, width), F32),
            pltpu.VMEM((rank, width), BF16),
            pltpu.VMEM((rank, width), BF16),
            pltpu.VMEM((tokens, width), BF16),
            pltpu.VMEM((tokens, width), BF16),
            pltpu.VMEM((max(BLOCK_ROWS), width), BF16),
            pltpu.VMEM((tokens, rank), BF16),
            pltpu.VMEM((tokens, rank), BF16),
            pltpu.VMEM((tokens, 1), F32),
            pltpu.VMEM((tokens, 1), F32),
            pltpu.VMEM((n * pad, LANES), F32),
            pltpu.VMEM((n, pad, LANES), BF16),
            pltpu.VMEM((n, pad, LANES), BF16),
            pltpu.VMEM((n, pad, LANES), F32),
            pltpu.VMEM((n, LANES), F32),
            pltpu.VMEM((n // 2, n, LANES), F32),
            pltpu.VMEM((n, LANES), F32),
            pltpu.SemaphoreType.DMA((3,)),
            pltpu.SemaphoreType.DMA((count,)),
            pltpu.SemaphoreType.DMA((count,)),
            pltpu.SemaphoreType.DMA((count,)),
            pltpu.SemaphoreType.DMA((count,)),
            pltpu.SemaphoreType.DMA((count,)),
            pltpu.SemaphoreType.DMA((n,)),
            pltpu.SemaphoreType.DMA((n,)),
            pltpu.SemaphoreType.DMA((n,)),
            pltpu.SemaphoreType.DMA((n,)),
        ],
        compiler_params=pltpu.CompilerParams(
            collective_id=0, has_side_effects=True, vmem_limit_bytes=40 * 2**20
        ),
        cost_estimate=pl.CostEstimate(
            flops=12 * tokens * width * rank, bytes_accessed=6 * tokens * width, transcendentals=0
        ),
    )(*[pltpu.with_memory_space_constraint(a, pltpu.HBM) for a in (activations, upstream, gain, down, up)])
    return pl.pallas_call(
        store_results,
        out_shape=shapes,
        in_specs=[anywhere, anywhere],
        out_specs=(anywhere, anywhere),
        scratch_shapes=[pltpu.SemaphoreType.DMA((PIECES + 1,))],
    )(*held)


def solution(mesh):
    return jax.shard_map(
        functools.partial(per_device, mesh.shape["section"], mesh.shape["dp"]),
        mesh=mesh,
        in_specs=(
            P("section", "dp", None),
            P("section", "dp", None),
            P("section", None),
            P("section", None, None),
            P("section", None, None),
        ),
        out_specs=(P("section", "dp", None), P("section", "dp")),
        check_vma=False,
    )
```

```python
import functools

import jax
import jax.numpy as jnp
from jax import lax
from jax.experimental import pallas as pl
from jax.experimental.pallas import tpu as pltpu
from jax.sharding import PartitionSpec as P

norm_eps = 1e-05
pair_eps = 1e-06
adapter_scale = 2.0
LANES = 128
MESH = pl.DeviceIdType.MESH
F32 = jnp.float32
BF16 = jnp.bfloat16

BLOCK_ROWS = (16, 16, 32, 64)
PIECES = 8
CHUNK = 1024


def contract_last(a, b):
    return lax.dot_general(a, b, (((1,), (1,)), ((), ())), preferred_element_type=F32)


def contract_first(a, b):
    return lax.dot_general(a, b, (((0,), (0,)), ((), ())), preferred_element_type=F32)


def tree_coefficients(gram, n):
    row = lax.broadcasted_iota(jnp.int32, (n, LANES), 0)
    lane = lax.broadcasted_iota(jnp.int32, (n, LANES), 1)
    same = row == lane
    coef = jnp.ones((n, 1), F32)
    step = 1
    while step < n:
        own = jnp.where(same, gram, 0.0)
        cross = jnp.where(lane == (row ^ step), gram, 0.0)

        def factor(axis):
            own_square = jnp.maximum(jnp.sum(own, axis=axis, keepdims=True), 0.0)
            inner = jnp.sum(cross, axis=axis, keepdims=True)
            return 1.0 - inner / (2.0 * (own_square + pair_eps))

        down, across = factor(1), factor(0)
        coef = coef * down
        gram = gram * down * across
        gram = gram + jnp.where(
            (row & step) != 0, pltpu.roll(gram, step, 0), pltpu.roll(gram, n - step, 0)
        )
        gram = gram + jnp.where(
            (lane & step) != 0, pltpu.roll(gram, step, 1), pltpu.roll(gram, LANES - step, 1)
        )
        step *= 2
    return coef


def kernel(
    sections, n, q, pad,
    x_hbm, g_hbm, gain_hbm, down_hbm, up_hbm,
    passed_ref, pair_ref,
    x_ref, g_ref, gain_ref, down_ref, up_ref, normed_ref, grad_ref, zero_ref,
    red_ref, low_ref,
    flat_ref, vsend, vrecv, vwide, gram_send, gram_recv, coef_ref,
    w_sem, x_sem, g_sem, zero_sem,
    pass_send, pass_recv, v_send_sem, v_recv_sem, gram_send_sem, gram_recv_sem,
    here_sem, round_sem, ready_sem,
):
    tokens, width = x_ref.shape
    rank = down_ref.shape[0]
    tiles = width // LANES
    half = n // 2
    section = lax.axis_index("section")
    me = lax.axis_index("dp")
    sends = section > 0
    receives = section < sections - 1
    before = lax.rem(section + sections - 1, sections)

    starts = [sum(BLOCK_ROWS[:b]) for b in range(len(BLOCK_ROWS))]
    blocks = [pl.ds(start, rows) for start, rows in zip(starts, BLOCK_ROWS)]

    weights = [
        pltpu.make_async_copy(up_hbm.at[0], up_ref, w_sem.at[0]),
        pltpu.make_async_copy(down_hbm.at[0], down_ref, w_sem.at[1]),
        pltpu.make_async_copy(gain_hbm, gain_ref, w_sem.at[2]),
    ]
    x_in = [pltpu.make_async_copy(x_hbm.at[0, r], x_ref.at[r], x_sem.at[b]) for b, r in enumerate(blocks)]
    g_in = [pltpu.make_async_copy(g_hbm.at[0, r], g_ref.at[r], g_sem.at[b]) for b, r in enumerate(blocks)]
    x_in[0].start()
    weights[0].start()
    g_in[0].start()
    weights[1].start()
    weights[2].start()
    for b in range(1, len(blocks)):
        x_in[b].start()
        g_in[b].start()

    barrier = pltpu.get_barrier_semaphore()

    def to_peers(semaphore):
        def signal(k, carry):
            pl.semaphore_signal(
                semaphore, inc=1, device_id=(section, lax.rem(me + k, n)), device_id_type=MESH
            )
            return carry

        lax.fori_loop(1, n, signal, 0)

    @pl.when(receives)
    def _():
        pl.semaphore_signal(barrier, inc=1, device_id=(section + 1, me), device_id_type=MESH)

    @pl.when(section == 0)
    def _():
        to_peers(barrier)

    def pass_copy(b):
        return pltpu.make_async_remote_copy(
            src_ref=grad_ref.at[blocks[b]],
            dst_ref=passed_ref.at[0, blocks[b]],
            send_sem=pass_send.at[b],
            recv_sem=pass_recv.at[b],
            device_id=(before, me),
            device_id_type=MESH,
        )

    def work(b):
        count = BLOCK_ROWS[b]
        rows = slice(starts[b], starts[b] + count)
        chunk = CHUNK if count <= 32 else CHUNK // 2
        columns = [slice(c, c + chunk) for c in range(0, width, chunk)]
        x_in[b].wait()
        g_in[b].wait()
        if b == 0:
            for copy in weights:
                copy.wait()
        low = jnp.zeros((count, rank), F32)
        for c in columns:
            low = low + contract_last(g_ref[rows, c], up_ref[:, c])
        low = (adapter_scale * low).astype(BF16)
        squares = jnp.zeros((count, LANES), F32)
        for c in range(0, width, LANES):
            wide = x_ref[rows, c : c + LANES].astype(F32)
            squares = squares + wide * wide
        inverse = lax.rsqrt(jnp.sum(squares, axis=1, keepdims=True) / width + norm_eps)
        red = jnp.zeros((count, rank), F32)
        for c in columns:
            normed = (x_ref[rows, c].astype(F32) * inverse * gain_ref[:, c]).astype(BF16)
            normed_ref[rows, c] = normed
            red = red + contract_last(normed, down_ref[:, c])
        low_ref[rows, :] = low
        red_ref[rows, :] = red.astype(BF16)
        shift = inverse * (jnp.sum(low.astype(F32) * red, axis=1, keepdims=True) / width)
        for c in columns:
            back = jnp.dot(low, down_ref[:, c], preferred_element_type=F32) * gain_ref[:, c]
            grad = g_ref[rows, c].astype(F32) + inverse * (back - x_ref[rows, c].astype(F32) * shift)
            grad_ref[rows, c] = grad.astype(BF16)

        @pl.when(sends)
        def _():
            if b == 0:
                pl.semaphore_wait(barrier, 1)
                pl.semaphore_signal(here_sem, inc=1, device_id=(before, me), device_id_type=MESH)
            pass_copy(b).start()

    work(0)

    @pl.when(jnp.logical_not(receives))
    def _():
        zero_ref[...] = jnp.zeros_like(zero_ref)
        for b, r in enumerate(blocks):
            pltpu.make_async_copy(
                zero_ref.at[pl.ds(0, BLOCK_ROWS[b])], passed_ref.at[0, r], zero_sem.at[b]
            ).start()

    for b in range(1, len(blocks)):
        work(b)

    @pl.when(section == 0)
    def _():
        pl.semaphore_wait(barrier, n - 1)

        @pl.when(receives)
        def _():
            pl.semaphore_wait(here_sem, 1)
            to_peers(round_sem)

    if pad != q:
        flat_ref[...] = jnp.zeros_like(flat_ref)
        stride = (tiles // q) * pad
    else:
        stride = tiles
    for c in range(0, width, CHUNK):
        down_term = contract_first(low_ref[...], normed_ref[:, c : c + CHUNK]) / tokens
        up_term = adapter_scale * contract_first(red_ref[...], g_ref[:, c : c + CHUNK]) / tokens
        for t, term in enumerate((down_term, up_term)):
            for inner in range(CHUNK // LANES):
                tile = c // LANES + inner
                place = tile if pad == q else (tile // q) * pad + tile % q
                flat_ref[pl.ds(t * half * pad + place, rank, stride=stride), :] = (
                    term[:, inner * LANES : (inner + 1) * LANES]
                )

    def pack(d, carry):
        vsend[d] = flat_ref[pl.ds(pl.multiple_of(d * pad, 8), pad), :].astype(BF16)
        return carry

    lax.fori_loop(0, n, pack, 0)

    @pl.when(sends)
    def _():
        pl.semaphore_wait(ready_sem, 1)

        @pl.when(receives)
        def _():
            pl.semaphore_wait(here_sem, 1)
            to_peers(round_sem)

    @pl.when(receives)
    def _():
        pl.semaphore_wait(round_sem, n - 1)
        pl.semaphore_signal(ready_sem, inc=1, device_id=(section + 1, me), device_id_type=MESH)

    def v_copy(k):
        to = lax.rem(me + k, n)
        return pltpu.make_async_remote_copy(
            src_ref=vsend.at[to],
            dst_ref=vrecv.at[me],
            send_sem=v_send_sem.at[k],
            recv_sem=v_recv_sem.at[k],
            device_id=(section, to),
            device_id_type=MESH,
        )

    def v_arrival(k):
        source = lax.rem(me + n - k, n)
        return pltpu.make_async_remote_copy(
            src_ref=vsend.at[source],
            dst_ref=vrecv.at[source],
            send_sem=v_send_sem.at[k],
            recv_sem=v_recv_sem.at[k],
            device_id=(section, source),
            device_id_type=MESH,
        )

    def v_start(k, carry):
        v_copy(k).start()
        return carry

    lax.fori_loop(1, n, v_start, 0)
    vwide[me] = vsend[me].astype(F32)

    def v_wait(k, carry):
        v_arrival(k).wait_recv()
        source = lax.rem(me + n - k, n)
        vwide[source] = vrecv[source].astype(F32)
        return carry

    lax.fori_loop(1, n, v_wait, 0)

    lane = lax.broadcasted_iota(jnp.int32, (n, LANES), 1)

    def gram_column(i, gram):
        products = jnp.sum(vwide[...] * vwide[i][None], axis=1)
        return jnp.where(lane == i, jnp.sum(products, axis=1, keepdims=True), gram)

    gram_send[...] = lax.fori_loop(0, n, gram_column, jnp.zeros((n, LANES), F32))

    base = (me // half) * half
    place = me - base

    def gram_copy(k):
        to = lax.rem(place + k, half)
        return pltpu.make_async_remote_copy(
            src_ref=gram_send,
            dst_ref=gram_recv.at[place],
            send_sem=gram_send_sem.at[k],
            recv_sem=gram_recv_sem.at[k],
            device_id=(section, base + to),
            device_id_type=MESH,
        )

    def gram_arrival(k):
        source = lax.rem(place + half - k, half)
        return pltpu.make_async_remote_copy(
            src_ref=gram_send,
            dst_ref=gram_recv.at[source],
            send_sem=gram_send_sem.at[k],
            recv_sem=gram_recv_sem.at[k],
            device_id=(section, base + source),
            device_id_type=MESH,
        )

    def gram_start(k, carry):
        gram_copy(k).start()
        return carry

    lax.fori_loop(1, half, gram_start, 0)
    gram_recv[place] = gram_send[...]

    def gram_wait(k, carry):
        gram_arrival(k).wait_recv()
        return carry

    lax.fori_loop(1, half, gram_wait, 0)

    coef = tree_coefficients(jnp.sum(gram_recv[...], axis=0), n)
    coef_ref[...] = jnp.broadcast_to(coef, (n, LANES))

    def weigh(i, total):
        return total + coef_ref[pl.ds(i, 1), :] * vwide[i]

    total = lax.fori_loop(0, n, weigh, jnp.zeros((pad, LANES), F32))
    for tile in range(q):
        pair_ref[:, tile * LANES : (tile + 1) * LANES] = total[tile : tile + 1, :].astype(BF16)

    def sent(k, carry):
        v_copy(k).wait_send()
        return carry

    lax.fori_loop(1, n, sent, 0)

    def gram_sent(k, carry):
        gram_copy(k).wait_send()
        return carry

    lax.fori_loop(1, half, gram_sent, 0)

    @pl.when(jnp.logical_not(receives))
    def _():
        for b, r in enumerate(blocks):
            pltpu.make_async_copy(
                zero_ref.at[pl.ds(0, BLOCK_ROWS[b])], passed_ref.at[0, r], zero_sem.at[b]
            ).wait()

    @pl.when(sends)
    def _():
        for b in range(len(blocks)):
            pass_copy(b).wait_send()

    @pl.when(receives)
    def _():
        for b in range(len(blocks)):
            pass_copy(b).wait_recv()


def store_results(passed_in, pair_in, passed_out, pair_out, sem):
    rows = passed_in.shape[1] // PIECES
    copies = [pltpu.make_async_copy(pair_in, pair_out, sem.at[PIECES])]
    for i in range(PIECES):
        piece = pl.ds(i * rows, rows)
        copies.append(pltpu.make_async_copy(passed_in.at[0, piece], passed_out.at[0, piece], sem.at[i]))
    for copy in copies:
        copy.start()
    for copy in copies:
        copy.wait()


def per_device(sections, n, activations, upstream, gain, down, up):
    _, tokens, width = activations.shape
    rank = down.shape[1]
    share = 2 * rank * width // n
    q = share // LANES
    pad = q if share >= width else -(-q // 16) * 16
    count = len(BLOCK_ROWS)
    anywhere = pl.BlockSpec(memory_space=pl.ANY)
    shapes = (
        jax.ShapeDtypeStruct(activations.shape, BF16),
        jax.ShapeDtypeStruct((1, share), BF16),
    )
    held = pl.pallas_call(
        functools.partial(kernel, sections, n, q, pad),
        out_shape=shapes,
        in_specs=[pl.BlockSpec(memory_space=pltpu.HBM)] * 5,
        out_specs=(anywhere, pl.BlockSpec(memory_space=pltpu.VMEM)),
        scratch_shapes=[
            pltpu.VMEM((tokens, width), BF16),
            pltpu.VMEM((tokens, width), BF16),
            pltpu.VMEM((1, width), F32),
            pltpu.VMEM((rank, width), BF16),
            pltpu.VMEM((rank, width), BF16),
            pltpu.VMEM((tokens, width), BF16),
            pltpu.VMEM((tokens, width), BF16),
            pltpu.VMEM((max(BLOCK_ROWS), width), BF16),
            pltpu.VMEM((tokens, rank), BF16),
            pltpu.VMEM((tokens, rank), BF16),
            pltpu.VMEM((n * pad, LANES), F32),
            pltpu.VMEM((n, pad, LANES), BF16),
            pltpu.VMEM((n, pad, LANES), BF16),
            pltpu.VMEM((n, pad, LANES), F32),
            pltpu.VMEM((n, LANES), F32),
            pltpu.VMEM((n // 2, n, LANES), F32),
            pltpu.VMEM((n, LANES), F32),
            pltpu.SemaphoreType.DMA((3,)),
            pltpu.SemaphoreType.DMA((count,)),
            pltpu.SemaphoreType.DMA((count,)),
            pltpu.SemaphoreType.DMA((count,)),
            pltpu.SemaphoreType.DMA((count,)),
            pltpu.SemaphoreType.DMA((count,)),
            pltpu.SemaphoreType.DMA((n,)),
            pltpu.SemaphoreType.DMA((n,)),
            pltpu.SemaphoreType.DMA((n,)),
            pltpu.SemaphoreType.DMA((n,)),
            pltpu.SemaphoreType.REGULAR,
            pltpu.SemaphoreType.REGULAR,
            pltpu.SemaphoreType.REGULAR,
        ],
        compiler_params=pltpu.CompilerParams(
            collective_id=0, has_side_effects=True, vmem_limit_bytes=40 * 2**20
        ),
        cost_estimate=pl.CostEstimate(
            flops=12 * tokens * width * rank, bytes_accessed=6 * tokens * width, transcendentals=0
        ),
    )(*[pltpu.with_memory_space_constraint(a, pltpu.HBM) for a in (activations, upstream, gain, down, up)])
    return pl.pallas_call(
        store_results,
        out_shape=shapes,
        in_specs=[pl.BlockSpec(memory_space=pltpu.VMEM)] * 2,
        out_specs=(anywhere, anywhere),
        scratch_shapes=[pltpu.SemaphoreType.DMA((PIECES + 1,))],
    )(*held)


def solution(mesh):
    return jax.shard_map(
        functools.partial(per_device, mesh.shape["section"], mesh.shape["dp"]),
        mesh=mesh,
        in_specs=(
            P("section", "dp", None),
            P("section", "dp", None),
            P("section", None),
            P("section", None, None),
            P("section", None, None),
        ),
        out_specs=(P("section", "dp", None), P("section", "dp")),
        check_vma=False,
    )
```

```python
import functools

import jax
import jax.numpy as jnp
from jax import lax
from jax.experimental import pallas as pl
from jax.experimental.pallas import tpu as pltpu
from jax.sharding import PartitionSpec as P

norm_eps = 1e-05
pair_eps = 1e-06
adapter_scale = 2.0
LANES = 128
MESH = pl.DeviceIdType.MESH
F32 = jnp.float32
BF16 = jnp.bfloat16

BLOCK_ROWS = (16, 16, 32, 64)
CHUNK = 1024


def contract_last(a, b):
    return lax.dot_general(a, b, (((1,), (1,)), ((), ())), preferred_element_type=F32)


def contract_first(a, b):
    return lax.dot_general(a, b, (((0,), (0,)), ((), ())), preferred_element_type=F32)


def tree_coefficients(gram, n):
    row = lax.broadcasted_iota(jnp.int32, (n, LANES), 0)
    lane = lax.broadcasted_iota(jnp.int32, (n, LANES), 1)
    same = row == lane
    coef = jnp.ones((n, 1), F32)
    step = 1
    while step < n:
        own = jnp.where(same, gram, 0.0)
        cross = jnp.where(lane == (row ^ step), gram, 0.0)

        def factor(axis):
            own_square = jnp.maximum(jnp.sum(own, axis=axis, keepdims=True), 0.0)
            inner = jnp.sum(cross, axis=axis, keepdims=True)
            return 1.0 - inner / (2.0 * (own_square + pair_eps))

        down, across = factor(1), factor(0)
        coef = coef * down
        gram = gram * down * across
        gram = gram + jnp.where(
            (row & step) != 0, pltpu.roll(gram, step, 0), pltpu.roll(gram, n - step, 0)
        )
        gram = gram + jnp.where(
            (lane & step) != 0, pltpu.roll(gram, step, 1), pltpu.roll(gram, LANES - step, 1)
        )
        step *= 2
    return coef


def kernel(
    sections, n, q, pad,
    x_hbm, g_hbm, gain_hbm, down_hbm, up_hbm,
    passed_ref, pair_ref,
    x_ref, g_ref, gain_ref, down_ref, up_ref, normed_ref, grad_ref, zero_ref,
    red_ref, low_ref,
    flat_ref, vsend, vrecv, vwide, gram_send, gram_recv, coef_ref,
    w_sem, x_sem, g_sem, zero_sem,
    pass_send, pass_recv, v_send_sem, v_recv_sem, gram_send_sem, gram_recv_sem,
    here_sem, round_sem, ready_sem,
):
    tokens, width = x_ref.shape
    rank = down_ref.shape[0]
    tiles = width // LANES
    half = n // 2
    section = lax.axis_index("section")
    me = lax.axis_index("dp")
    sends = section > 0
    receives = section < sections - 1
    before = lax.rem(section + sections - 1, sections)

    starts = [sum(BLOCK_ROWS[:b]) for b in range(len(BLOCK_ROWS))]
    blocks = [pl.ds(start, rows) for start, rows in zip(starts, BLOCK_ROWS)]

    weights = [
        pltpu.make_async_copy(up_hbm.at[0], up_ref, w_sem.at[0]),
        pltpu.make_async_copy(down_hbm.at[0], down_ref, w_sem.at[1]),
        pltpu.make_async_copy(gain_hbm, gain_ref, w_sem.at[2]),
    ]
    x_in = [pltpu.make_async_copy(x_hbm.at[0, r], x_ref.at[r], x_sem.at[b]) for b, r in enumerate(blocks)]
    g_in = [pltpu.make_async_copy(g_hbm.at[0, r], g_ref.at[r], g_sem.at[b]) for b, r in enumerate(blocks)]
    x_in[0].start()
    g_in[0].start()
    for copy in weights:
        copy.start()

    barrier = pltpu.get_barrier_semaphore()

    def to_peers(semaphore):
        def signal(k, carry):
            pl.semaphore_signal(
                semaphore, inc=1, device_id=(section, lax.rem(me + k, n)), device_id_type=MESH
            )
            return carry

        lax.fori_loop(1, n, signal, 0)

    @pl.when(receives)
    def _():
        pl.semaphore_signal(barrier, inc=1, device_id=(section + 1, me), device_id_type=MESH)

    @pl.when(section == 0)
    def _():
        to_peers(barrier)

    def pass_copy(b):
        return pltpu.make_async_remote_copy(
            src_ref=grad_ref.at[blocks[b]],
            dst_ref=passed_ref.at[0, blocks[b]],
            send_sem=pass_send.at[b],
            recv_sem=pass_recv.at[b],
            device_id=(before, me),
            device_id_type=MESH,
        )

    def work(b):
        count = BLOCK_ROWS[b]
        rows = slice(starts[b], starts[b] + count)
        chunk = CHUNK if count <= 32 else CHUNK // 2
        columns = [slice(c, c + chunk) for c in range(0, width, chunk)]
        x_in[b].wait()
        g_in[b].wait()
        if b == 0:
            for copy in weights:
                copy.wait()
            for later in range(1, len(blocks)):
                x_in[later].start()
                g_in[later].start()
        low = jnp.zeros((count, rank), F32)
        for c in columns:
            low = low + contract_last(g_ref[rows, c], up_ref[:, c])
        low = (adapter_scale * low).astype(BF16)
        squares = jnp.zeros((count, LANES), F32)
        for c in range(0, width, LANES):
            wide = x_ref[rows, c : c + LANES].astype(F32)
            squares = squares + wide * wide
        inverse = lax.rsqrt(jnp.sum(squares, axis=1, keepdims=True) / width + norm_eps)
        red = jnp.zeros((count, rank), F32)
        for c in columns:
            normed = (x_ref[rows, c].astype(F32) * inverse * gain_ref[:, c]).astype(BF16)
            normed_ref[rows, c] = normed
            red = red + contract_last(normed, down_ref[:, c])
        low_ref[rows, :] = low
        red_ref[rows, :] = red.astype(BF16)
        shift = inverse * (jnp.sum(low.astype(F32) * red, axis=1, keepdims=True) / width)
        for c in columns:
            back = jnp.dot(low, down_ref[:, c], preferred_element_type=F32) * gain_ref[:, c]
            grad = g_ref[rows, c].astype(F32) + inverse * (back - x_ref[rows, c].astype(F32) * shift)
            grad_ref[rows, c] = grad.astype(BF16)

        @pl.when(sends)
        def _():
            if b == 0:
                pl.semaphore_wait(barrier, 1)
                pl.semaphore_signal(here_sem, inc=1, device_id=(before, me), device_id_type=MESH)
            pass_copy(b).start()

    work(0)

    @pl.when(jnp.logical_not(receives))
    def _():
        zero_ref[...] = jnp.zeros_like(zero_ref)
        for b, r in enumerate(blocks):
            pltpu.make_async_copy(
                zero_ref.at[pl.ds(0, BLOCK_ROWS[b])], passed_ref.at[0, r], zero_sem.at[b]
            ).start()

    for b in range(1, len(blocks)):
        work(b)

    @pl.when(section == 0)
    def _():
        pl.semaphore_wait(barrier, n - 1)

        @pl.when(receives)
        def _():
            pl.semaphore_wait(here_sem, 1)
            to_peers(round_sem)

    if pad != q:
        flat_ref[...] = jnp.zeros_like(flat_ref)
        stride = (tiles // q) * pad
    else:
        stride = tiles
    for c in range(0, width, CHUNK):
        down_term = contract_first(low_ref[...], normed_ref[:, c : c + CHUNK]) / tokens
        up_term = adapter_scale * contract_first(red_ref[...], g_ref[:, c : c + CHUNK]) / tokens
        for t, term in enumerate((down_term, up_term)):
            for inner in range(CHUNK // LANES):
                tile = c // LANES + inner
                place = tile if pad == q else (tile // q) * pad + tile % q
                flat_ref[pl.ds(t * half * pad + place, rank, stride=stride), :] = (
                    term[:, inner * LANES : (inner + 1) * LANES]
                )

    def pack(d, carry):
        vsend[d] = flat_ref[pl.ds(pl.multiple_of(d * pad, 8), pad), :].astype(BF16)
        return carry

    lax.fori_loop(0, n, pack, 0)

    @pl.when(sends)
    def _():
        pl.semaphore_wait(ready_sem, 1)

        @pl.when(receives)
        def _():
            pl.semaphore_wait(here_sem, 1)
            to_peers(round_sem)

    @pl.when(receives)
    def _():
        pl.semaphore_wait(round_sem, n - 1)
        pl.semaphore_signal(ready_sem, inc=1, device_id=(section + 1, me), device_id_type=MESH)

    def v_copy(k):
        to = lax.rem(me + k, n)
        return pltpu.make_async_remote_copy(
            src_ref=vsend.at[to],
            dst_ref=vrecv.at[me],
            send_sem=v_send_sem.at[k],
            recv_sem=v_recv_sem.at[k],
            device_id=(section, to),
            device_id_type=MESH,
        )

    def v_arrival(k):
        source = lax.rem(me + n - k, n)
        return pltpu.make_async_remote_copy(
            src_ref=vsend.at[source],
            dst_ref=vrecv.at[source],
            send_sem=v_send_sem.at[k],
            recv_sem=v_recv_sem.at[k],
            device_id=(section, source),
            device_id_type=MESH,
        )

    def v_start(k, carry):
        v_copy(k).start()
        return carry

    lax.fori_loop(1, n, v_start, 0)
    vwide[me] = vsend[me].astype(F32)

    def v_wait(k, carry):
        v_arrival(k).wait_recv()
        source = lax.rem(me + n - k, n)
        vwide[source] = vrecv[source].astype(F32)
        return carry

    lax.fori_loop(1, n, v_wait, 0)

    lane = lax.broadcasted_iota(jnp.int32, (n, LANES), 1)

    def gram_column(i, gram):
        products = jnp.sum(vwide[...] * vwide[i][None], axis=1)
        return jnp.where(lane == i, jnp.sum(products, axis=1, keepdims=True), gram)

    gram_send[...] = lax.fori_loop(0, n, gram_column, jnp.zeros((n, LANES), F32))

    base = (me // half) * half
    place = me - base

    def gram_copy(k):
        to = lax.rem(place + k, half)
        return pltpu.make_async_remote_copy(
            src_ref=gram_send,
            dst_ref=gram_recv.at[place],
            send_sem=gram_send_sem.at[k],
            recv_sem=gram_recv_sem.at[k],
            device_id=(section, base + to),
            device_id_type=MESH,
        )

    def gram_arrival(k):
        source = lax.rem(place + half - k, half)
        return pltpu.make_async_remote_copy(
            src_ref=gram_send,
            dst_ref=gram_recv.at[source],
            send_sem=gram_send_sem.at[k],
            recv_sem=gram_recv_sem.at[k],
            device_id=(section, base + source),
            device_id_type=MESH,
        )

    def gram_start(k, carry):
        gram_copy(k).start()
        return carry

    lax.fori_loop(1, half, gram_start, 0)
    gram_recv[place] = gram_send[...]

    def gram_wait(k, carry):
        gram_arrival(k).wait_recv()
        return carry

    lax.fori_loop(1, half, gram_wait, 0)

    coef = tree_coefficients(jnp.sum(gram_recv[...], axis=0), n)
    coef_ref[...] = jnp.broadcast_to(coef, (n, LANES))

    def weigh(i, total):
        return total + coef_ref[pl.ds(i, 1), :] * vwide[i]

    total = lax.fori_loop(0, n, weigh, jnp.zeros((pad, LANES), F32))
    for tile in range(q):
        pair_ref[:, tile * LANES : (tile + 1) * LANES] = total[tile : tile + 1, :].astype(BF16)

    def sent(k, carry):
        v_copy(k).wait_send()
        return carry

    lax.fori_loop(1, n, sent, 0)

    def gram_sent(k, carry):
        gram_copy(k).wait_send()
        return carry

    lax.fori_loop(1, half, gram_sent, 0)

    @pl.when(jnp.logical_not(receives))
    def _():
        for b, r in enumerate(blocks):
            pltpu.make_async_copy(
                zero_ref.at[pl.ds(0, BLOCK_ROWS[b])], passed_ref.at[0, r], zero_sem.at[b]
            ).wait()

    @pl.when(sends)
    def _():
        for b in range(len(blocks)):
            pass_copy(b).wait_send()

    @pl.when(receives)
    def _():
        for b in range(len(blocks)):
            pass_copy(b).wait_recv()


def per_device(sections, n, activations, upstream, gain, down, up):
    _, tokens, width = activations.shape
    rank = down.shape[1]
    share = 2 * rank * width // n
    q = share // LANES
    pad = q if share >= width else -(-q // 16) * 16
    count = len(BLOCK_ROWS)
    anywhere = pl.BlockSpec(memory_space=pl.ANY)
    shapes = (
        jax.ShapeDtypeStruct(activations.shape, BF16),
        jax.ShapeDtypeStruct((1, share), BF16),
    )
    return pl.pallas_call(
        functools.partial(kernel, sections, n, q, pad),
        out_shape=shapes,
        in_specs=[pl.BlockSpec(memory_space=pltpu.HBM)] * 5,
        out_specs=(anywhere, pl.BlockSpec(memory_space=pltpu.VMEM)),
        scratch_shapes=[
            pltpu.VMEM((tokens, width), BF16),
            pltpu.VMEM((tokens, width), BF16),
            pltpu.VMEM((1, width), F32),
            pltpu.VMEM((rank, width), BF16),
            pltpu.VMEM((rank, width), BF16),
            pltpu.VMEM((tokens, width), BF16),
            pltpu.VMEM((tokens, width), BF16),
            pltpu.VMEM((max(BLOCK_ROWS), width), BF16),
            pltpu.VMEM((tokens, rank), BF16),
            pltpu.VMEM((tokens, rank), BF16),
            pltpu.VMEM((n * pad, LANES), F32),
            pltpu.VMEM((n, pad, LANES), BF16),
            pltpu.VMEM((n, pad, LANES), BF16),
            pltpu.VMEM((n, pad, LANES), F32),
            pltpu.VMEM((n, LANES), F32),
            pltpu.VMEM((n // 2, n, LANES), F32),
            pltpu.VMEM((n, LANES), F32),
            pltpu.SemaphoreType.DMA((3,)),
            pltpu.SemaphoreType.DMA((count,)),
            pltpu.SemaphoreType.DMA((count,)),
            pltpu.SemaphoreType.DMA((count,)),
            pltpu.SemaphoreType.DMA((count,)),
            pltpu.SemaphoreType.DMA((count,)),
            pltpu.SemaphoreType.DMA((n,)),
            pltpu.SemaphoreType.DMA((n,)),
            pltpu.SemaphoreType.DMA((n,)),
            pltpu.SemaphoreType.DMA((n,)),
            pltpu.SemaphoreType.REGULAR,
            pltpu.SemaphoreType.REGULAR,
            pltpu.SemaphoreType.REGULAR,
        ],
        compiler_params=pltpu.CompilerParams(
            collective_id=0, has_side_effects=True, vmem_limit_bytes=40 * 2**20
        ),
        cost_estimate=pl.CostEstimate(
            flops=12 * tokens * width * rank, bytes_accessed=6 * tokens * width, transcendentals=0
        ),
    )(*[pltpu.with_memory_space_constraint(a, pltpu.HBM) for a in (activations, upstream, gain, down, up)])


def solution(mesh):
    return jax.shard_map(
        functools.partial(per_device, mesh.shape["section"], mesh.shape["dp"]),
        mesh=mesh,
        in_specs=(
            P("section", "dp", None),
            P("section", "dp", None),
            P("section", None),
            P("section", None, None),
            P("section", None, None),
        ),
        out_specs=(P("section", "dp", None), P("section", "dp")),
        check_vma=False,
    )
```

```python
import functools

import jax
import jax.numpy as jnp
from jax import lax
from jax.experimental import pallas as pl
from jax.experimental.pallas import tpu as pltpu
from jax.sharding import PartitionSpec as P

norm_eps = 1e-05
pair_eps = 1e-06
adapter_scale = 2.0
LANES = 128
MESH = pl.DeviceIdType.MESH
F32 = jnp.float32
BF16 = jnp.bfloat16

BLOCK_ROWS = (16, 16, 32, 64)
CHUNK = 1024
PIECES = 8


def contract_last(a, b):
    return lax.dot_general(a, b, (((1,), (1,)), ((), ())), preferred_element_type=F32)


def contract_first(a, b):
    return lax.dot_general(a, b, (((0,), (0,)), ((), ())), preferred_element_type=F32)


def tree_coefficients(gram, n):
    row = lax.broadcasted_iota(jnp.int32, (n, LANES), 0)
    lane = lax.broadcasted_iota(jnp.int32, (n, LANES), 1)
    same = row == lane
    coef = jnp.ones((n, 1), F32)
    step = 1
    while step < n:
        own = jnp.where(same, gram, 0.0)
        cross = jnp.where(lane == (row ^ step), gram, 0.0)

        def factor(axis):
            own_square = jnp.maximum(jnp.sum(own, axis=axis, keepdims=True), 0.0)
            inner = jnp.sum(cross, axis=axis, keepdims=True)
            return 1.0 - inner / (2.0 * (own_square + pair_eps))

        down, across = factor(1), factor(0)
        coef = coef * down
        gram = gram * down * across
        gram = gram + jnp.where(
            (row & step) != 0, pltpu.roll(gram, step, 0), pltpu.roll(gram, n - step, 0)
        )
        gram = gram + jnp.where(
            (lane & step) != 0, pltpu.roll(gram, step, 1), pltpu.roll(gram, LANES - step, 1)
        )
        step *= 2
    return coef


def kernel(
    sections, n, q, pad,
    x_hbm, g_hbm, gain_hbm, down_hbm, up_hbm,
    passed_ref, pair_ref,
    x_ref, g_ref, gain_ref, down_ref, up_ref, normed_ref, grad_ref, zero_ref,
    red_ref, low_ref,
    flat_ref, vsend, vrecv, vwide, gram_send, gram_recv, coef_ref,
    w_sem, x_sem, g_sem, zero_sem,
    pass_send, pass_recv, v_send_sem, v_recv_sem, gram_send_sem, gram_recv_sem,
    here_sem, round_sem, ready_sem,
):
    tokens, width = x_ref.shape
    rank = down_ref.shape[0]
    tiles = width // LANES
    half = n // 2
    section = lax.axis_index("section")
    me = lax.axis_index("dp")
    sends = section > 0
    receives = section < sections - 1
    before = lax.rem(section + sections - 1, sections)

    starts = [sum(BLOCK_ROWS[:b]) for b in range(len(BLOCK_ROWS))]
    blocks = [pl.ds(start, rows) for start, rows in zip(starts, BLOCK_ROWS)]

    weights = [
        pltpu.make_async_copy(up_hbm.at[0], up_ref, w_sem.at[0]),
        pltpu.make_async_copy(down_hbm.at[0], down_ref, w_sem.at[1]),
        pltpu.make_async_copy(gain_hbm, gain_ref, w_sem.at[2]),
    ]
    x_in = [pltpu.make_async_copy(x_hbm.at[0, r], x_ref.at[r], x_sem.at[b]) for b, r in enumerate(blocks)]
    g_in = [pltpu.make_async_copy(g_hbm.at[0, r], g_ref.at[r], g_sem.at[b]) for b, r in enumerate(blocks)]
    x_in[0].start()
    g_in[0].start()
    for copy in weights:
        copy.start()

    barrier = pltpu.get_barrier_semaphore()

    def to_peers(semaphore):
        def signal(k, carry):
            pl.semaphore_signal(
                semaphore, inc=1, device_id=(section, lax.rem(me + k, n)), device_id_type=MESH
            )
            return carry

        lax.fori_loop(1, n, signal, 0)

    @pl.when(receives)
    def _():
        pl.semaphore_signal(barrier, inc=1, device_id=(section + 1, me), device_id_type=MESH)

    @pl.when(section == 0)
    def _():
        to_peers(barrier)

    def pass_copy(b):
        return pltpu.make_async_remote_copy(
            src_ref=grad_ref.at[blocks[b]],
            dst_ref=passed_ref.at[0, blocks[b]],
            send_sem=pass_send.at[b],
            recv_sem=pass_recv.at[b],
            device_id=(before, me),
            device_id_type=MESH,
        )

    def work(b):
        count = BLOCK_ROWS[b]
        rows = slice(starts[b], starts[b] + count)
        chunk = CHUNK if count <= 32 else CHUNK // 2
        columns = [slice(c, c + chunk) for c in range(0, width, chunk)]
        x_in[b].wait()
        g_in[b].wait()
        if b == 0:
            for copy in weights:
                copy.wait()
            for later in range(1, len(blocks)):
                x_in[later].start()
                g_in[later].start()
        low = jnp.zeros((count, rank), F32)
        for c in columns:
            low = low + contract_last(g_ref[rows, c], up_ref[:, c])
        low = (adapter_scale * low).astype(BF16)
        squares = jnp.zeros((count, LANES), F32)
        for c in range(0, width, LANES):
            wide = x_ref[rows, c : c + LANES].astype(F32)
            squares = squares + wide * wide
        inverse = lax.rsqrt(jnp.sum(squares, axis=1, keepdims=True) / width + norm_eps)
        red = jnp.zeros((count, rank), F32)
        for c in columns:
            normed = (x_ref[rows, c].astype(F32) * inverse * gain_ref[:, c]).astype(BF16)
            normed_ref[rows, c] = normed
            red = red + contract_last(normed, down_ref[:, c])
        low_ref[rows, :] = low
        red_ref[rows, :] = red.astype(BF16)
        shift = inverse * (jnp.sum(low.astype(F32) * red, axis=1, keepdims=True) / width)
        for c in columns:
            back = jnp.dot(low, down_ref[:, c], preferred_element_type=F32) * gain_ref[:, c]
            grad = g_ref[rows, c].astype(F32) + inverse * (back - x_ref[rows, c].astype(F32) * shift)
            grad_ref[rows, c] = grad.astype(BF16)

        @pl.when(sends)
        def _():
            if b == 0:
                pl.semaphore_wait(barrier, 1)
                pl.semaphore_signal(here_sem, inc=1, device_id=(before, me), device_id_type=MESH)
            pass_copy(b).start()

    work(0)

    @pl.when(jnp.logical_not(receives))
    def _():
        zero_ref[...] = jnp.zeros_like(zero_ref)
        for b, r in enumerate(blocks):
            pltpu.make_async_copy(
                zero_ref.at[pl.ds(0, BLOCK_ROWS[b])], passed_ref.at[0, r], zero_sem.at[b]
            ).start()

    for b in range(1, len(blocks)):
        work(b)

    @pl.when(section == 0)
    def _():
        pl.semaphore_wait(barrier, n - 1)

        @pl.when(receives)
        def _():
            pl.semaphore_wait(here_sem, 1)
            to_peers(round_sem)

    if pad != q:
        flat_ref[...] = jnp.zeros_like(flat_ref)
        stride = (tiles // q) * pad
    else:
        stride = tiles
    for c in range(0, width, CHUNK):
        down_term = contract_first(low_ref[...], normed_ref[:, c : c + CHUNK]) / tokens
        up_term = adapter_scale * contract_first(red_ref[...], g_ref[:, c : c + CHUNK]) / tokens
        for t, term in enumerate((down_term, up_term)):
            for inner in range(CHUNK // LANES):
                tile = c // LANES + inner
                place = tile if pad == q else (tile // q) * pad + tile % q
                flat_ref[pl.ds(t * half * pad + place, rank, stride=stride), :] = (
                    term[:, inner * LANES : (inner + 1) * LANES]
                )

    def pack(d, carry):
        vsend[d] = flat_ref[pl.ds(pl.multiple_of(d * pad, 8), pad), :].astype(BF16)
        return carry

    lax.fori_loop(0, n, pack, 0)

    @pl.when(sends)
    def _():
        pl.semaphore_wait(ready_sem, 1)

        @pl.when(receives)
        def _():
            pl.semaphore_wait(here_sem, 1)
            to_peers(round_sem)

    @pl.when(receives)
    def _():
        pl.semaphore_wait(round_sem, n - 1)
        pl.semaphore_signal(ready_sem, inc=1, device_id=(section + 1, me), device_id_type=MESH)

    def v_copy(k):
        to = lax.rem(me + k, n)
        return pltpu.make_async_remote_copy(
            src_ref=vsend.at[to],
            dst_ref=vrecv.at[me],
            send_sem=v_send_sem.at[k],
            recv_sem=v_recv_sem.at[k],
            device_id=(section, to),
            device_id_type=MESH,
        )

    def v_arrival(k):
        source = lax.rem(me + n - k, n)
        return pltpu.make_async_remote_copy(
            src_ref=vsend.at[source],
            dst_ref=vrecv.at[source],
            send_sem=v_send_sem.at[k],
            recv_sem=v_recv_sem.at[k],
            device_id=(section, source),
            device_id_type=MESH,
        )

    def v_start(k, carry):
        v_copy(k).start()
        return carry

    lax.fori_loop(1, n, v_start, 0)
    vwide[me] = vsend[me].astype(F32)

    def v_wait(k, carry):
        v_arrival(k).wait_recv()
        source = lax.rem(me + n - k, n)
        vwide[source] = vrecv[source].astype(F32)
        return carry

    lax.fori_loop(1, n, v_wait, 0)

    lane = lax.broadcasted_iota(jnp.int32, (n, LANES), 1)

    def gram_column(i, gram):
        products = jnp.sum(vwide[...] * vwide[i][None], axis=1)
        return jnp.where(lane == i, jnp.sum(products, axis=1, keepdims=True), gram)

    gram_send[...] = lax.fori_loop(0, n, gram_column, jnp.zeros((n, LANES), F32))

    base = (me // half) * half
    place = me - base

    def gram_copy(k):
        to = lax.rem(place + k, half)
        return pltpu.make_async_remote_copy(
            src_ref=gram_send,
            dst_ref=gram_recv.at[place],
            send_sem=gram_send_sem.at[k],
            recv_sem=gram_recv_sem.at[k],
            device_id=(section, base + to),
            device_id_type=MESH,
        )

    def gram_arrival(k):
        source = lax.rem(place + half - k, half)
        return pltpu.make_async_remote_copy(
            src_ref=gram_send,
            dst_ref=gram_recv.at[source],
            send_sem=gram_send_sem.at[k],
            recv_sem=gram_recv_sem.at[k],
            device_id=(section, base + source),
            device_id_type=MESH,
        )

    def gram_start(k, carry):
        gram_copy(k).start()
        return carry

    lax.fori_loop(1, half, gram_start, 0)
    gram_recv[place] = gram_send[...]

    def gram_wait(k, carry):
        gram_arrival(k).wait_recv()
        return carry

    lax.fori_loop(1, half, gram_wait, 0)

    coef = tree_coefficients(jnp.sum(gram_recv[...], axis=0), n)
    coef_ref[...] = jnp.broadcast_to(coef, (n, LANES))

    def weigh(i, total):
        return total + coef_ref[pl.ds(i, 1), :] * vwide[i]

    total = lax.fori_loop(0, n, weigh, jnp.zeros((pad, LANES), F32))
    for tile in range(q):
        pair_ref[:, tile * LANES : (tile + 1) * LANES] = total[tile : tile + 1, :].astype(BF16)

    def sent(k, carry):
        v_copy(k).wait_send()
        return carry

    lax.fori_loop(1, n, sent, 0)

    def gram_sent(k, carry):
        gram_copy(k).wait_send()
        return carry

    lax.fori_loop(1, half, gram_sent, 0)

    @pl.when(jnp.logical_not(receives))
    def _():
        for b, r in enumerate(blocks):
            pltpu.make_async_copy(
                zero_ref.at[pl.ds(0, BLOCK_ROWS[b])], passed_ref.at[0, r], zero_sem.at[b]
            ).wait()

    @pl.when(sends)
    def _():
        for b in range(len(blocks)):
            pass_copy(b).wait_send()

    @pl.when(receives)
    def _():
        for b in range(len(blocks)):
            pass_copy(b).wait_recv()


def store_results(passed_in, pair_in, passed_out, pair_out, sem):
    rows = passed_in.shape[1] // PIECES
    copies = [pltpu.make_async_copy(pair_in, pair_out, sem.at[PIECES])]
    for i in range(PIECES):
        piece = pl.ds(i * rows, rows)
        copies.append(pltpu.make_async_copy(passed_in.at[0, piece], passed_out.at[0, piece], sem.at[i]))
    for copy in copies:
        copy.start()
    for copy in copies:
        copy.wait()


def per_device(sections, n, activations, upstream, gain, down, up):
    _, tokens, width = activations.shape
    rank = down.shape[1]
    share = 2 * rank * width // n
    q = share // LANES
    pad = q if share >= width else -(-q // 16) * 16
    count = len(BLOCK_ROWS)
    anywhere = pl.BlockSpec(memory_space=pl.ANY)
    shapes = (
        jax.ShapeDtypeStruct(activations.shape, BF16),
        jax.ShapeDtypeStruct((1, share), BF16),
    )
    held = pl.pallas_call(
        functools.partial(kernel, sections, n, q, pad),
        out_shape=shapes,
        in_specs=[pl.BlockSpec(memory_space=pltpu.HBM)] * 5,
        out_specs=(anywhere, pl.BlockSpec(memory_space=pltpu.VMEM)),
        scratch_shapes=[
            pltpu.VMEM((tokens, width), BF16),
            pltpu.VMEM((tokens, width), BF16),
            pltpu.VMEM((1, width), F32),
            pltpu.VMEM((rank, width), BF16),
            pltpu.VMEM((rank, width), BF16),
            pltpu.VMEM((tokens, width), BF16),
            pltpu.VMEM((tokens, width), BF16),
            pltpu.VMEM((max(BLOCK_ROWS), width), BF16),
            pltpu.VMEM((tokens, rank), BF16),
            pltpu.VMEM((tokens, rank), BF16),
            pltpu.VMEM((n * pad, LANES), F32),
            pltpu.VMEM((n, pad, LANES), BF16),
            pltpu.VMEM((n, pad, LANES), BF16),
            pltpu.VMEM((n, pad, LANES), F32),
            pltpu.VMEM((n, LANES), F32),
            pltpu.VMEM((n // 2, n, LANES), F32),
            pltpu.VMEM((n, LANES), F32),
            pltpu.SemaphoreType.DMA((3,)),
            pltpu.SemaphoreType.DMA((count,)),
            pltpu.SemaphoreType.DMA((count,)),
            pltpu.SemaphoreType.DMA((count,)),
            pltpu.SemaphoreType.DMA((count,)),
            pltpu.SemaphoreType.DMA((count,)),
            pltpu.SemaphoreType.DMA((n,)),
            pltpu.SemaphoreType.DMA((n,)),
            pltpu.SemaphoreType.DMA((n,)),
            pltpu.SemaphoreType.DMA((n,)),
            pltpu.SemaphoreType.REGULAR,
            pltpu.SemaphoreType.REGULAR,
            pltpu.SemaphoreType.REGULAR,
        ],
        compiler_params=pltpu.CompilerParams(
            collective_id=0, has_side_effects=True, vmem_limit_bytes=40 * 2**20
        ),
        cost_estimate=pl.CostEstimate(
            flops=12 * tokens * width * rank, bytes_accessed=6 * tokens * width, transcendentals=0
        ),
    )(*[pltpu.with_memory_space_constraint(a, pltpu.HBM) for a in (activations, upstream, gain, down, up)])
    return pl.pallas_call(
        store_results,
        out_shape=shapes,
        in_specs=[anywhere, anywhere],
        out_specs=(anywhere, anywhere),
        scratch_shapes=[pltpu.SemaphoreType.DMA((PIECES + 1,))],
    )(*[pltpu.with_memory_space_constraint(value, pltpu.VMEM) for value in held])


def solution(mesh):
    return jax.shard_map(
        functools.partial(per_device, mesh.shape["section"], mesh.shape["dp"]),
        mesh=mesh,
        in_specs=(
            P("section", "dp", None),
            P("section", "dp", None),
            P("section", None),
            P("section", None, None),
            P("section", None, None),
        ),
        out_specs=(P("section", "dp", None), P("section", "dp")),
        check_vma=False,
    )
```

```python
import functools

import jax
import jax.numpy as jnp
from jax import lax
from jax.experimental import pallas as pl
from jax.experimental.pallas import tpu as pltpu
from jax.sharding import PartitionSpec as P

norm_eps = 1e-05
pair_eps = 1e-06
adapter_scale = 2.0
LANES = 128
MESH = pl.DeviceIdType.MESH
F32 = jnp.float32
BF16 = jnp.bfloat16

BLOCK_ROWS = (16, 16, 32, 64)
CHUNK = 1024
PIECES = 8
SEND_ROWS = 16


def contract_last(a, b):
    return lax.dot_general(a, b, (((1,), (1,)), ((), ())), preferred_element_type=F32)


def contract_first(a, b):
    return lax.dot_general(a, b, (((0,), (0,)), ((), ())), preferred_element_type=F32)


def tree_coefficients(gram, n):
    row = lax.broadcasted_iota(jnp.int32, (n, LANES), 0)
    lane = lax.broadcasted_iota(jnp.int32, (n, LANES), 1)
    same = row == lane
    coef = jnp.ones((n, 1), F32)
    step = 1
    while step < n:
        own = jnp.where(same, gram, 0.0)
        cross = jnp.where(lane == (row ^ step), gram, 0.0)

        def factor(axis):
            own_square = jnp.maximum(jnp.sum(own, axis=axis, keepdims=True), 0.0)
            inner = jnp.sum(cross, axis=axis, keepdims=True)
            return 1.0 - inner / (2.0 * (own_square + pair_eps))

        down, across = factor(1), factor(0)
        coef = coef * down
        gram = gram * down * across
        gram = gram + jnp.where(
            (row & step) != 0, pltpu.roll(gram, step, 0), pltpu.roll(gram, n - step, 0)
        )
        gram = gram + jnp.where(
            (lane & step) != 0, pltpu.roll(gram, step, 1), pltpu.roll(gram, LANES - step, 1)
        )
        step *= 2
    return coef


def kernel(
    sections, n, q, pad,
    x_hbm, g_hbm, gain_hbm, down_hbm, up_hbm,
    passed_ref, pair_ref,
    x_ref, g_ref, gain_ref, down_ref, up_ref, normed_ref, grad_ref, zero_ref,
    red_ref, low_ref,
    flat_ref, vsend, vrecv, vwide, gram_send, gram_recv, coef_ref,
    w_sem, x_sem, g_sem, zero_sem,
    pass_send, pass_recv, v_send_sem, v_recv_sem, gram_send_sem, gram_recv_sem,
    here_sem, round_sem, ready_sem,
):
    tokens, width = x_ref.shape
    rank = down_ref.shape[0]
    tiles = width // LANES
    half = n // 2
    section = lax.axis_index("section")
    me = lax.axis_index("dp")
    sends = section > 0
    receives = section < sections - 1
    before = lax.rem(section + sections - 1, sections)

    starts = [sum(BLOCK_ROWS[:b]) for b in range(len(BLOCK_ROWS))]
    blocks = [pl.ds(start, rows) for start, rows in zip(starts, BLOCK_ROWS)]

    weights = [
        pltpu.make_async_copy(up_hbm.at[0], up_ref, w_sem.at[0]),
        pltpu.make_async_copy(down_hbm.at[0], down_ref, w_sem.at[1]),
        pltpu.make_async_copy(gain_hbm, gain_ref, w_sem.at[2]),
    ]
    x_in = [pltpu.make_async_copy(x_hbm.at[0, r], x_ref.at[r], x_sem.at[b]) for b, r in enumerate(blocks)]
    g_in = [pltpu.make_async_copy(g_hbm.at[0, r], g_ref.at[r], g_sem.at[b]) for b, r in enumerate(blocks)]
    x_in[0].start()
    g_in[0].start()
    for copy in weights:
        copy.start()

    barrier = pltpu.get_barrier_semaphore()

    def to_peers(semaphore):
        def signal(k, carry):
            pl.semaphore_signal(
                semaphore, inc=1, device_id=(section, lax.rem(me + k, n)), device_id_type=MESH
            )
            return carry

        lax.fori_loop(1, n, signal, 0)

    @pl.when(receives)
    def _():
        pl.semaphore_signal(barrier, inc=1, device_id=(section + 1, me), device_id_type=MESH)

    @pl.when(section == 0)
    def _():
        to_peers(barrier)

    def pass_copy(i):
        rows = pl.ds(i * SEND_ROWS, SEND_ROWS)
        return pltpu.make_async_remote_copy(
            src_ref=grad_ref.at[rows],
            dst_ref=passed_ref.at[0, rows],
            send_sem=pass_send.at[i],
            recv_sem=pass_recv.at[i],
            device_id=(before, me),
            device_id_type=MESH,
        )

    def work(b):
        count = BLOCK_ROWS[b]
        rows = slice(starts[b], starts[b] + count)
        chunk = CHUNK if count <= 32 else CHUNK // 2
        columns = [slice(c, c + chunk) for c in range(0, width, chunk)]
        x_in[b].wait()
        g_in[b].wait()
        if b == 0:
            for copy in weights:
                copy.wait()
            for later in range(1, len(blocks)):
                x_in[later].start()
                g_in[later].start()
        low = jnp.zeros((count, rank), F32)
        for c in columns:
            low = low + contract_last(g_ref[rows, c], up_ref[:, c])
        low = (adapter_scale * low).astype(BF16)
        squares = jnp.zeros((count, LANES), F32)
        for c in range(0, width, LANES):
            wide = x_ref[rows, c : c + LANES].astype(F32)
            squares = squares + wide * wide
        inverse = lax.rsqrt(jnp.sum(squares, axis=1, keepdims=True) / width + norm_eps)
        red = jnp.zeros((count, rank), F32)
        for c in columns:
            normed = (x_ref[rows, c].astype(F32) * inverse * gain_ref[:, c]).astype(BF16)
            normed_ref[rows, c] = normed
            red = red + contract_last(normed, down_ref[:, c])
        low_ref[rows, :] = low
        red_ref[rows, :] = red.astype(BF16)
        shift = inverse * (jnp.sum(low.astype(F32) * red, axis=1, keepdims=True) / width)
        for c in columns:
            back = jnp.dot(low, down_ref[:, c], preferred_element_type=F32) * gain_ref[:, c]
            grad = g_ref[rows, c].astype(F32) + inverse * (back - x_ref[rows, c].astype(F32) * shift)
            grad_ref[rows, c] = grad.astype(BF16)

        @pl.when(sends)
        def _():
            if b == 0:
                pl.semaphore_wait(barrier, 1)
                pl.semaphore_signal(here_sem, inc=1, device_id=(before, me), device_id_type=MESH)
            for i in range(starts[b] // SEND_ROWS, (starts[b] + count) // SEND_ROWS):
                pass_copy(i).start()

    work(0)

    @pl.when(jnp.logical_not(receives))
    def _():
        zero_ref[...] = jnp.zeros_like(zero_ref)
        for b, r in enumerate(blocks):
            pltpu.make_async_copy(
                zero_ref.at[pl.ds(0, BLOCK_ROWS[b])], passed_ref.at[0, r], zero_sem.at[b]
            ).start()

    for b in range(1, len(blocks)):
        work(b)

    @pl.when(section == 0)
    def _():
        pl.semaphore_wait(barrier, n - 1)

        @pl.when(receives)
        def _():
            pl.semaphore_wait(here_sem, 1)
            to_peers(round_sem)

    if pad != q:
        flat_ref[...] = jnp.zeros_like(flat_ref)
        stride = (tiles // q) * pad
    else:
        stride = tiles
    for c in range(0, width, CHUNK):
        down_term = contract_first(low_ref[...], normed_ref[:, c : c + CHUNK]) / tokens
        up_term = adapter_scale * contract_first(red_ref[...], g_ref[:, c : c + CHUNK]) / tokens
        for t, term in enumerate((down_term, up_term)):
            for inner in range(CHUNK // LANES):
                tile = c // LANES + inner
                place = tile if pad == q else (tile // q) * pad + tile % q
                flat_ref[pl.ds(t * half * pad + place, rank, stride=stride), :] = (
                    term[:, inner * LANES : (inner + 1) * LANES]
                )

    def pack(d, carry):
        vsend[d] = flat_ref[pl.ds(pl.multiple_of(d * pad, 8), pad), :].astype(BF16)
        return carry

    lax.fori_loop(0, n, pack, 0)

    @pl.when(sends)
    def _():
        pl.semaphore_wait(ready_sem, 1)

        @pl.when(receives)
        def _():
            pl.semaphore_wait(here_sem, 1)
            to_peers(round_sem)

    @pl.when(receives)
    def _():
        pl.semaphore_wait(round_sem, n - 1)
        pl.semaphore_signal(ready_sem, inc=1, device_id=(section + 1, me), device_id_type=MESH)

    def v_copy(k):
        to = lax.rem(me + k, n)
        return pltpu.make_async_remote_copy(
            src_ref=vsend.at[to],
            dst_ref=vrecv.at[me],
            send_sem=v_send_sem.at[k],
            recv_sem=v_recv_sem.at[k],
            device_id=(section, to),
            device_id_type=MESH,
        )

    def v_arrival(k):
        source = lax.rem(me + n - k, n)
        return pltpu.make_async_remote_copy(
            src_ref=vsend.at[source],
            dst_ref=vrecv.at[source],
            send_sem=v_send_sem.at[k],
            recv_sem=v_recv_sem.at[k],
            device_id=(section, source),
            device_id_type=MESH,
        )

    def v_start(k, carry):
        v_copy(k).start()
        return carry

    lax.fori_loop(1, n, v_start, 0)
    vwide[me] = vsend[me].astype(F32)

    def v_wait(k, carry):
        v_arrival(k).wait_recv()
        source = lax.rem(me + n - k, n)
        vwide[source] = vrecv[source].astype(F32)
        return carry

    lax.fori_loop(1, n, v_wait, 0)

    lane = lax.broadcasted_iota(jnp.int32, (n, LANES), 1)

    def gram_column(i, gram):
        products = jnp.sum(vwide[...] * vwide[i][None], axis=1)
        return jnp.where(lane == i, jnp.sum(products, axis=1, keepdims=True), gram)

    gram_send[...] = lax.fori_loop(0, n, gram_column, jnp.zeros((n, LANES), F32))

    base = (me // half) * half
    place = me - base

    def gram_copy(k):
        to = lax.rem(place + k, half)
        return pltpu.make_async_remote_copy(
            src_ref=gram_send,
            dst_ref=gram_recv.at[place],
            send_sem=gram_send_sem.at[k],
            recv_sem=gram_recv_sem.at[k],
            device_id=(section, base + to),
            device_id_type=MESH,
        )

    def gram_arrival(k):
        source = lax.rem(place + half - k, half)
        return pltpu.make_async_remote_copy(
            src_ref=gram_send,
            dst_ref=gram_recv.at[source],
            send_sem=gram_send_sem.at[k],
            recv_sem=gram_recv_sem.at[k],
            device_id=(section, base + source),
            device_id_type=MESH,
        )

    def gram_start(k, carry):
        gram_copy(k).start()
        return carry

    lax.fori_loop(1, half, gram_start, 0)
    gram_recv[place] = gram_send[...]

    def gram_wait(k, carry):
        gram_arrival(k).wait_recv()
        return carry

    lax.fori_loop(1, half, gram_wait, 0)

    coef = tree_coefficients(jnp.sum(gram_recv[...], axis=0), n)
    coef_ref[...] = jnp.broadcast_to(coef, (n, LANES))

    def weigh(i, total):
        return total + coef_ref[pl.ds(i, 1), :] * vwide[i]

    total = lax.fori_loop(0, n, weigh, jnp.zeros((pad, LANES), F32))
    for tile in range(q):
        pair_ref[:, tile * LANES : (tile + 1) * LANES] = total[tile : tile + 1, :].astype(BF16)

    def sent(k, carry):
        v_copy(k).wait_send()
        return carry

    lax.fori_loop(1, n, sent, 0)

    def gram_sent(k, carry):
        gram_copy(k).wait_send()
        return carry

    lax.fori_loop(1, half, gram_sent, 0)

    @pl.when(jnp.logical_not(receives))
    def _():
        for b, r in enumerate(blocks):
            pltpu.make_async_copy(
                zero_ref.at[pl.ds(0, BLOCK_ROWS[b])], passed_ref.at[0, r], zero_sem.at[b]
            ).wait()

    @pl.when(sends)
    def _():
        for i in range(tokens // SEND_ROWS):
            pass_copy(i).wait_send()

    @pl.when(receives)
    def _():
        for i in range(tokens // SEND_ROWS):
            pass_copy(i).wait_recv()


def store_results(passed_in, pair_in, passed_out, pair_out, sem):
    rows = passed_in.shape[1] // PIECES
    copies = [pltpu.make_async_copy(pair_in, pair_out, sem.at[PIECES])]
    for i in range(PIECES):
        piece = pl.ds(i * rows, rows)
        copies.append(pltpu.make_async_copy(passed_in.at[0, piece], passed_out.at[0, piece], sem.at[i]))
    for copy in copies:
        copy.start()
    for copy in copies:
        copy.wait()


def per_device(sections, n, activations, upstream, gain, down, up):
    _, tokens, width = activations.shape
    rank = down.shape[1]
    share = 2 * rank * width // n
    q = share // LANES
    pad = q if share >= width else -(-q // 16) * 16
    count = len(BLOCK_ROWS)
    anywhere = pl.BlockSpec(memory_space=pl.ANY)
    shapes = (
        jax.ShapeDtypeStruct(activations.shape, BF16),
        jax.ShapeDtypeStruct((1, share), BF16),
    )
    held = pl.pallas_call(
        functools.partial(kernel, sections, n, q, pad),
        out_shape=shapes,
        in_specs=[pl.BlockSpec(memory_space=pltpu.HBM)] * 5,
        out_specs=(anywhere, pl.BlockSpec(memory_space=pltpu.VMEM)),
        scratch_shapes=[
            pltpu.VMEM((tokens, width), BF16),
            pltpu.VMEM((tokens, width), BF16),
            pltpu.VMEM((1, width), F32),
            pltpu.VMEM((rank, width), BF16),
            pltpu.VMEM((rank, width), BF16),
            pltpu.VMEM((tokens, width), BF16),
            pltpu.VMEM((tokens, width), BF16),
            pltpu.VMEM((max(BLOCK_ROWS), width), BF16),
            pltpu.VMEM((tokens, rank), BF16),
            pltpu.VMEM((tokens, rank), BF16),
            pltpu.VMEM((n * pad, LANES), F32),
            pltpu.VMEM((n, pad, LANES), BF16),
            pltpu.VMEM((n, pad, LANES), BF16),
            pltpu.VMEM((n, pad, LANES), F32),
            pltpu.VMEM((n, LANES), F32),
            pltpu.VMEM((n // 2, n, LANES), F32),
            pltpu.VMEM((n, LANES), F32),
            pltpu.SemaphoreType.DMA((3,)),
            pltpu.SemaphoreType.DMA((count,)),
            pltpu.SemaphoreType.DMA((count,)),
            pltpu.SemaphoreType.DMA((count,)),
            pltpu.SemaphoreType.DMA((tokens // SEND_ROWS,)),
            pltpu.SemaphoreType.DMA((tokens // SEND_ROWS,)),
            pltpu.SemaphoreType.DMA((n,)),
            pltpu.SemaphoreType.DMA((n,)),
            pltpu.SemaphoreType.DMA((n,)),
            pltpu.SemaphoreType.DMA((n,)),
            pltpu.SemaphoreType.REGULAR,
            pltpu.SemaphoreType.REGULAR,
            pltpu.SemaphoreType.REGULAR,
        ],
        compiler_params=pltpu.CompilerParams(
            collective_id=0, has_side_effects=True, vmem_limit_bytes=40 * 2**20
        ),
        cost_estimate=pl.CostEstimate(
            flops=12 * tokens * width * rank, bytes_accessed=6 * tokens * width, transcendentals=0
        ),
    )(*[pltpu.with_memory_space_constraint(a, pltpu.HBM) for a in (activations, upstream, gain, down, up)])
    return pl.pallas_call(
        store_results,
        out_shape=shapes,
        in_specs=[anywhere, anywhere],
        out_specs=(anywhere, anywhere),
        scratch_shapes=[pltpu.SemaphoreType.DMA((PIECES + 1,))],
    )(*[pltpu.with_memory_space_constraint(value, pltpu.VMEM) for value in held])


def solution(mesh):
    return jax.shard_map(
        functools.partial(per_device, mesh.shape["section"], mesh.shape["dp"]),
        mesh=mesh,
        in_specs=(
            P("section", "dp", None),
            P("section", "dp", None),
            P("section", None),
            P("section", None, None),
            P("section", None, None),
        ),
        out_specs=(P("section", "dp", None), P("section", "dp")),
        check_vma=False,
    )
```

```python
import functools

import jax
import jax.numpy as jnp
from jax import lax
from jax.experimental import pallas as pl
from jax.experimental.pallas import tpu as pltpu
from jax.sharding import PartitionSpec as P

norm_eps = 1e-05
pair_eps = 1e-06
adapter_scale = 2.0
LANES = 128
MESH = pl.DeviceIdType.MESH
F32 = jnp.float32
BF16 = jnp.bfloat16

BLOCK_ROWS = (16, 16, 32, 64)
CHUNK = 1024
PIECES = 4


def contract_last(a, b):
    return lax.dot_general(a, b, (((1,), (1,)), ((), ())), preferred_element_type=F32)


def contract_first(a, b):
    return lax.dot_general(a, b, (((0,), (0,)), ((), ())), preferred_element_type=F32)


def tree_coefficients(gram, n):
    row = lax.broadcasted_iota(jnp.int32, (n, LANES), 0)
    lane = lax.broadcasted_iota(jnp.int32, (n, LANES), 1)
    same = row == lane
    coef = jnp.ones((n, 1), F32)
    step = 1
    while step < n:
        own = jnp.where(same, gram, 0.0)
        cross = jnp.where(lane == (row ^ step), gram, 0.0)

        def factor(axis):
            own_square = jnp.maximum(jnp.sum(own, axis=axis, keepdims=True), 0.0)
            inner = jnp.sum(cross, axis=axis, keepdims=True)
            return 1.0 - inner / (2.0 * (own_square + pair_eps))

        down, across = factor(1), factor(0)
        coef = coef * down
        gram = gram * down * across
        gram = gram + jnp.where(
            (row & step) != 0, pltpu.roll(gram, step, 0), pltpu.roll(gram, n - step, 0)
        )
        gram = gram + jnp.where(
            (lane & step) != 0, pltpu.roll(gram, step, 1), pltpu.roll(gram, LANES - step, 1)
        )
        step *= 2
    return coef


def kernel(
    sections, n, q, pad,
    x_hbm, g_hbm, gain_hbm, down_hbm, up_hbm,
    passed_ref, pair_ref,
    x_ref, g_ref, gain_ref, down_ref, up_ref, normed_ref, grad_ref, zero_ref,
    red_ref, low_ref,
    flat_ref, vsend, vrecv, vwide, gram_send, gram_recv, coef_ref,
    w_sem, x_sem, g_sem, zero_sem,
    pass_send, pass_recv, v_send_sem, v_recv_sem, gram_send_sem, gram_recv_sem,
    here_sem, round_sem, ready_sem,
):
    tokens, width = x_ref.shape
    rank = down_ref.shape[0]
    tiles = width // LANES
    half = n // 2
    section = lax.axis_index("section")
    me = lax.axis_index("dp")
    sends = section > 0
    receives = section < sections - 1
    before = lax.rem(section + sections - 1, sections)

    starts = [sum(BLOCK_ROWS[:b]) for b in range(len(BLOCK_ROWS))]
    blocks = [pl.ds(start, rows) for start, rows in zip(starts, BLOCK_ROWS)]

    weights = [
        pltpu.make_async_copy(up_hbm.at[0], up_ref, w_sem.at[0]),
        pltpu.make_async_copy(down_hbm.at[0], down_ref, w_sem.at[1]),
        pltpu.make_async_copy(gain_hbm, gain_ref, w_sem.at[2]),
    ]
    x_in = [pltpu.make_async_copy(x_hbm.at[0, r], x_ref.at[r], x_sem.at[b]) for b, r in enumerate(blocks)]
    g_in = [pltpu.make_async_copy(g_hbm.at[0, r], g_ref.at[r], g_sem.at[b]) for b, r in enumerate(blocks)]
    x_in[0].start()
    g_in[0].start()
    for copy in weights:
        copy.start()

    barrier = pltpu.get_barrier_semaphore()

    def to_peers(semaphore):
        def signal(k, carry):
            pl.semaphore_signal(
                semaphore, inc=1, device_id=(section, lax.rem(me + k, n)), device_id_type=MESH
            )
            return carry

        lax.fori_loop(1, n, signal, 0)

    @pl.when(receives)
    def _():
        pl.semaphore_signal(barrier, inc=1, device_id=(section + 1, me), device_id_type=MESH)

    @pl.when(section == 0)
    def _():
        to_peers(barrier)

    def pass_copy(b):
        return pltpu.make_async_remote_copy(
            src_ref=grad_ref.at[blocks[b]],
            dst_ref=passed_ref.at[0, blocks[b]],
            send_sem=pass_send.at[b],
            recv_sem=pass_recv.at[b],
            device_id=(before, me),
            device_id_type=MESH,
        )

    def work(b):
        count = BLOCK_ROWS[b]
        rows = slice(starts[b], starts[b] + count)
        chunk = CHUNK if count <= 32 else CHUNK // 2
        columns = [slice(c, c + chunk) for c in range(0, width, chunk)]
        spans = columns if count > 16 else [slice(0, width)]
        x_in[b].wait()
        g_in[b].wait()
        if b == 0:
            for copy in weights:
                copy.wait()
            for later in range(1, len(blocks)):
                x_in[later].start()
                g_in[later].start()
        low = jnp.zeros((count, rank), F32)
        for c in spans:
            low = low + contract_last(g_ref[rows, c], up_ref[:, c])
        low = (adapter_scale * low).astype(BF16)
        squares = jnp.zeros((count, LANES), F32)
        for c in range(0, width, LANES):
            wide = x_ref[rows, c : c + LANES].astype(F32)
            squares = squares + wide * wide
        inverse = lax.rsqrt(jnp.sum(squares, axis=1, keepdims=True) / width + norm_eps)
        red = jnp.zeros((count, rank), F32)
        for c in spans:
            normed = (x_ref[rows, c].astype(F32) * inverse * gain_ref[:, c]).astype(BF16)
            normed_ref[rows, c] = normed
            red = red + contract_last(normed, down_ref[:, c])
        low_ref[rows, :] = low
        red_ref[rows, :] = red.astype(BF16)
        shift = inverse * (jnp.sum(low.astype(F32) * red, axis=1, keepdims=True) / width)
        for c in columns:
            back = jnp.dot(low, down_ref[:, c], preferred_element_type=F32) * gain_ref[:, c]
            grad = g_ref[rows, c].astype(F32) + inverse * (back - x_ref[rows, c].astype(F32) * shift)
            grad_ref[rows, c] = grad.astype(BF16)

        @pl.when(sends)
        def _():
            if b == 0:
                pl.semaphore_wait(barrier, 1)
            pass_copy(b).start()
            if b == 0:
                pl.semaphore_signal(here_sem, inc=1, device_id=(before, me), device_id_type=MESH)

    work(0)

    @pl.when(jnp.logical_not(receives))
    def _():
        zero_ref[...] = jnp.zeros_like(zero_ref)
        for b, r in enumerate(blocks):
            pltpu.make_async_copy(
                zero_ref.at[pl.ds(0, BLOCK_ROWS[b])], passed_ref.at[0, r], zero_sem.at[b]
            ).start()

    for b in range(1, len(blocks)):
        work(b)

    @pl.when(section == 0)
    def _():
        pl.semaphore_wait(barrier, n - 1)

        @pl.when(receives)
        def _():
            pl.semaphore_wait(here_sem, 1)
            to_peers(round_sem)

    if pad != q:
        flat_ref[...] = jnp.zeros_like(flat_ref)
        stride = (tiles // q) * pad
    else:
        stride = tiles
    for c in range(0, width, CHUNK):
        down_term = contract_first(low_ref[...], normed_ref[:, c : c + CHUNK]) / tokens
        up_term = adapter_scale * contract_first(red_ref[...], g_ref[:, c : c + CHUNK]) / tokens
        for t, term in enumerate((down_term, up_term)):
            for inner in range(CHUNK // LANES):
                tile = c // LANES + inner
                place = tile if pad == q else (tile // q) * pad + tile % q
                flat_ref[pl.ds(t * half * pad + place, rank, stride=stride), :] = (
                    term[:, inner * LANES : (inner + 1) * LANES]
                )

    def pack(d, carry):
        vsend[d] = flat_ref[pl.ds(pl.multiple_of(d * pad, 8), pad), :].astype(BF16)
        return carry

    lax.fori_loop(0, n, pack, 0)

    @pl.when(sends)
    def _():
        pl.semaphore_wait(ready_sem, 1)

        @pl.when(receives)
        def _():
            pl.semaphore_wait(here_sem, 1)
            to_peers(round_sem)

    @pl.when(receives)
    def _():
        pl.semaphore_wait(round_sem, n - 1)
        pl.semaphore_signal(ready_sem, inc=1, device_id=(section + 1, me), device_id_type=MESH)

    def v_copy(k):
        to = lax.rem(me + k, n)
        return pltpu.make_async_remote_copy(
            src_ref=vsend.at[to],
            dst_ref=vrecv.at[me],
            send_sem=v_send_sem.at[k],
            recv_sem=v_recv_sem.at[k],
            device_id=(section, to),
            device_id_type=MESH,
        )

    def v_arrival(k):
        source = lax.rem(me + n - k, n)
        return pltpu.make_async_remote_copy(
            src_ref=vsend.at[source],
            dst_ref=vrecv.at[source],
            send_sem=v_send_sem.at[k],
            recv_sem=v_recv_sem.at[k],
            device_id=(section, source),
            device_id_type=MESH,
        )

    def v_start(k, carry):
        v_copy(k).start()
        return carry

    lax.fori_loop(1, n, v_start, 0)
    vwide[me] = vsend[me].astype(F32)

    def v_wait(k, carry):
        v_arrival(k).wait_recv()
        source = lax.rem(me + n - k, n)
        vwide[source] = vrecv[source].astype(F32)
        return carry

    lax.fori_loop(1, n, v_wait, 0)

    lane = lax.broadcasted_iota(jnp.int32, (n, LANES), 1)

    def gram_column(i, gram):
        products = jnp.sum(vwide[...] * vwide[i][None], axis=1)
        return jnp.where(lane == i, jnp.sum(products, axis=1, keepdims=True), gram)

    gram_send[...] = lax.fori_loop(0, n, gram_column, jnp.zeros((n, LANES), F32))

    base = (me // half) * half
    place = me - base

    def gram_copy(k):
        to = lax.rem(place + k, half)
        return pltpu.make_async_remote_copy(
            src_ref=gram_send,
            dst_ref=gram_recv.at[place],
            send_sem=gram_send_sem.at[k],
            recv_sem=gram_recv_sem.at[k],
            device_id=(section, base + to),
            device_id_type=MESH,
        )

    def gram_arrival(k):
        source = lax.rem(place + half - k, half)
        return pltpu.make_async_remote_copy(
            src_ref=gram_send,
            dst_ref=gram_recv.at[source],
            send_sem=gram_send_sem.at[k],
            recv_sem=gram_recv_sem.at[k],
            device_id=(section, base + source),
            device_id_type=MESH,
        )

    def gram_start(k, carry):
        gram_copy(k).start()
        return carry

    lax.fori_loop(1, half, gram_start, 0)
    gram_recv[place] = gram_send[...]

    def gram_wait(k, carry):
        gram_arrival(k).wait_recv()
        return carry

    lax.fori_loop(1, half, gram_wait, 0)

    coef = tree_coefficients(jnp.sum(gram_recv[...], axis=0), n)
    coef_ref[...] = jnp.broadcast_to(coef, (n, LANES))

    def weigh(i, total):
        return total + coef_ref[pl.ds(i, 1), :] * vwide[i]

    total = lax.fori_loop(0, n, weigh, jnp.zeros((pad, LANES), F32))
    for tile in range(q):
        pair_ref[:, tile * LANES : (tile + 1) * LANES] = total[tile : tile + 1, :].astype(BF16)

    def sent(k, carry):
        v_copy(k).wait_send()
        return carry

    lax.fori_loop(1, n, sent, 0)

    def gram_sent(k, carry):
        gram_copy(k).wait_send()
        return carry

    lax.fori_loop(1, half, gram_sent, 0)

    @pl.when(jnp.logical_not(receives))
    def _():
        for b, r in enumerate(blocks):
            pltpu.make_async_copy(
                zero_ref.at[pl.ds(0, BLOCK_ROWS[b])], passed_ref.at[0, r], zero_sem.at[b]
            ).wait()

    @pl.when(sends)
    def _():
        for b in range(len(blocks)):
            pass_copy(b).wait_send()

    @pl.when(receives)
    def _():
        for b in range(len(blocks)):
            pass_copy(b).wait_recv()


def store_results(passed_in, pair_in, passed_out, pair_out, sem):
    rows = passed_in.shape[1] // PIECES
    copies = [pltpu.make_async_copy(pair_in, pair_out, sem.at[PIECES])]
    for i in range(PIECES):
        piece = pl.ds(i * rows, rows)
        copies.append(pltpu.make_async_copy(passed_in.at[0, piece], passed_out.at[0, piece], sem.at[i]))
    for copy in copies:
        copy.start()
    for copy in copies:
        copy.wait()


def per_device(sections, n, activations, upstream, gain, down, up):
    _, tokens, width = activations.shape
    rank = down.shape[1]
    share = 2 * rank * width // n
    q = share // LANES
    pad = q if share >= width else -(-q // 16) * 16
    count = len(BLOCK_ROWS)
    anywhere = pl.BlockSpec(memory_space=pl.ANY)
    shapes = (
        jax.ShapeDtypeStruct(activations.shape, BF16),
        jax.ShapeDtypeStruct((1, share), BF16),
    )
    held = pl.pallas_call(
        functools.partial(kernel, sections, n, q, pad),
        out_shape=shapes,
        in_specs=[pl.BlockSpec(memory_space=pltpu.HBM)] * 5,
        out_specs=(anywhere, pl.BlockSpec(memory_space=pltpu.VMEM)),
        scratch_shapes=[
            pltpu.VMEM((tokens, width), BF16),
            pltpu.VMEM((tokens, width), BF16),
            pltpu.VMEM((1, width), F32),
            pltpu.VMEM((rank, width), BF16),
            pltpu.VMEM((rank, width), BF16),
            pltpu.VMEM((tokens, width), BF16),
            pltpu.VMEM((tokens, width), BF16),
            pltpu.VMEM((max(BLOCK_ROWS), width), BF16),
            pltpu.VMEM((tokens, rank), BF16),
            pltpu.VMEM((tokens, rank), BF16),
            pltpu.VMEM((n * pad, LANES), F32),
            pltpu.VMEM((n, pad, LANES), BF16),
            pltpu.VMEM((n, pad, LANES), BF16),
            pltpu.VMEM((n, pad, LANES), F32),
            pltpu.VMEM((n, LANES), F32),
            pltpu.VMEM((n // 2, n, LANES), F32),
            pltpu.VMEM((n, LANES), F32),
            pltpu.SemaphoreType.DMA((3,)),
            pltpu.SemaphoreType.DMA((count,)),
            pltpu.SemaphoreType.DMA((count,)),
            pltpu.SemaphoreType.DMA((count,)),
            pltpu.SemaphoreType.DMA((count,)),
            pltpu.SemaphoreType.DMA((count,)),
            pltpu.SemaphoreType.DMA((n,)),
            pltpu.SemaphoreType.DMA((n,)),
            pltpu.SemaphoreType.DMA((n,)),
            pltpu.SemaphoreType.DMA((n,)),
            pltpu.SemaphoreType.REGULAR,
            pltpu.SemaphoreType.REGULAR,
            pltpu.SemaphoreType.REGULAR,
        ],
        compiler_params=pltpu.CompilerParams(
            collective_id=0, has_side_effects=True, vmem_limit_bytes=40 * 2**20
        ),
        cost_estimate=pl.CostEstimate(
            flops=12 * tokens * width * rank, bytes_accessed=6 * tokens * width, transcendentals=0
        ),
    )(*[pltpu.with_memory_space_constraint(a, pltpu.HBM) for a in (activations, upstream, gain, down, up)])
    return pl.pallas_call(
        store_results,
        out_shape=shapes,
        in_specs=[anywhere, anywhere],
        out_specs=(anywhere, anywhere),
        scratch_shapes=[pltpu.SemaphoreType.DMA((PIECES + 1,))],
    )(*[pltpu.with_memory_space_constraint(value, pltpu.VMEM) for value in held])


def solution(mesh):
    return jax.shard_map(
        functools.partial(per_device, mesh.shape["section"], mesh.shape["dp"]),
        mesh=mesh,
        in_specs=(
            P("section", "dp", None),
            P("section", "dp", None),
            P("section", None),
            P("section", None, None),
            P("section", None, None),
        ),
        out_specs=(P("section", "dp", None), P("section", "dp")),
        check_vma=False,
    )
```

```python
import functools

import jax
import jax.numpy as jnp
from jax import lax
from jax.experimental import pallas as pl
from jax.experimental.pallas import tpu as pltpu
from jax.sharding import PartitionSpec as P

norm_eps = 1e-05
pair_eps = 1e-06
adapter_scale = 2.0
LANES = 128
MESH = pl.DeviceIdType.MESH
F32 = jnp.float32
BF16 = jnp.bfloat16

BLOCK_ROWS = (16, 48, 64)
CHUNK = 1024
PIECES = 4


def contract_last(a, b):
    return lax.dot_general(a, b, (((1,), (1,)), ((), ())), preferred_element_type=F32)


def contract_first(a, b):
    return lax.dot_general(a, b, (((0,), (0,)), ((), ())), preferred_element_type=F32)


def tree_coefficients(gram, n):
    row = lax.broadcasted_iota(jnp.int32, (n, LANES), 0)
    lane = lax.broadcasted_iota(jnp.int32, (n, LANES), 1)
    same = row == lane
    coef = jnp.ones((n, 1), F32)
    step = 1
    while step < n:
        own = jnp.where(same, gram, 0.0)
        cross = jnp.where(lane == (row ^ step), gram, 0.0)

        def factor(axis):
            own_square = jnp.maximum(jnp.sum(own, axis=axis, keepdims=True), 0.0)
            inner = jnp.sum(cross, axis=axis, keepdims=True)
            return 1.0 - inner / (2.0 * (own_square + pair_eps))

        down, across = factor(1), factor(0)
        coef = coef * down
        gram = gram * down * across
        gram = gram + jnp.where(
            (row & step) != 0, pltpu.roll(gram, step, 0), pltpu.roll(gram, n - step, 0)
        )
        gram = gram + jnp.where(
            (lane & step) != 0, pltpu.roll(gram, step, 1), pltpu.roll(gram, LANES - step, 1)
        )
        step *= 2
    return coef


def kernel(
    sections, n, q, pad,
    x_hbm, g_hbm, gain_hbm, down_hbm, up_hbm,
    passed_ref, pair_ref,
    x_ref, g_ref, gain_ref, down_ref, up_ref, normed_ref, grad_ref, zero_ref,
    red_ref, low_ref,
    flat_ref, vsend, vrecv, vwide, gram_send, gram_recv, coef_ref,
    w_sem, x_sem, g_sem, zero_sem,
    pass_send, pass_recv, v_send_sem, v_recv_sem, gram_send_sem, gram_recv_sem,
    here_sem, round_sem, ready_sem,
):
    tokens, width = x_ref.shape
    rank = down_ref.shape[0]
    tiles = width // LANES
    half = n // 2
    section = lax.axis_index("section")
    me = lax.axis_index("dp")
    sends = section > 0
    receives = section < sections - 1
    before = lax.rem(section + sections - 1, sections)

    starts = [sum(BLOCK_ROWS[:b]) for b in range(len(BLOCK_ROWS))]
    blocks = [pl.ds(start, rows) for start, rows in zip(starts, BLOCK_ROWS)]

    weights = [
        pltpu.make_async_copy(up_hbm.at[0], up_ref, w_sem.at[0]),
        pltpu.make_async_copy(down_hbm.at[0], down_ref, w_sem.at[1]),
        pltpu.make_async_copy(gain_hbm, gain_ref, w_sem.at[2]),
    ]
    x_in = [pltpu.make_async_copy(x_hbm.at[0, r], x_ref.at[r], x_sem.at[b]) for b, r in enumerate(blocks)]
    g_in = [pltpu.make_async_copy(g_hbm.at[0, r], g_ref.at[r], g_sem.at[b]) for b, r in enumerate(blocks)]
    x_in[0].start()
    g_in[0].start()
    for copy in weights:
        copy.start()

    barrier = pltpu.get_barrier_semaphore()

    def to_peers(semaphore):
        def signal(k, carry):
            pl.semaphore_signal(
                semaphore, inc=1, device_id=(section, lax.rem(me + k, n)), device_id_type=MESH
            )
            return carry

        lax.fori_loop(1, n, signal, 0)

    @pl.when(receives)
    def _():
        pl.semaphore_signal(barrier, inc=1, device_id=(section + 1, me), device_id_type=MESH)

    @pl.when(section == 0)
    def _():
        to_peers(barrier)

    def pass_copy(b):
        return pltpu.make_async_remote_copy(
            src_ref=grad_ref.at[blocks[b]],
            dst_ref=passed_ref.at[0, blocks[b]],
            send_sem=pass_send.at[b],
            recv_sem=pass_recv.at[b],
            device_id=(before, me),
            device_id_type=MESH,
        )

    def work(b):
        count = BLOCK_ROWS[b]
        rows = slice(starts[b], starts[b] + count)
        chunk = CHUNK if count <= 32 else CHUNK // 2
        columns = [slice(c, c + chunk) for c in range(0, width, chunk)]
        spans = columns if count > 16 else [slice(0, width)]
        x_in[b].wait()
        g_in[b].wait()
        if b == 0:
            for copy in weights:
                copy.wait()
            for later in range(1, len(blocks)):
                x_in[later].start()
                g_in[later].start()
        low = jnp.zeros((count, rank), F32)
        for c in spans:
            low = low + contract_last(g_ref[rows, c], up_ref[:, c])
        low = (adapter_scale * low).astype(BF16)
        squares = jnp.zeros((count, LANES), F32)
        for c in range(0, width, LANES):
            wide = x_ref[rows, c : c + LANES].astype(F32)
            squares = squares + wide * wide
        inverse = lax.rsqrt(jnp.sum(squares, axis=1, keepdims=True) / width + norm_eps)
        red = jnp.zeros((count, rank), F32)
        for c in spans:
            normed = (x_ref[rows, c].astype(F32) * inverse * gain_ref[:, c]).astype(BF16)
            normed_ref[rows, c] = normed
            red = red + contract_last(normed, down_ref[:, c])
        low_ref[rows, :] = low
        red_ref[rows, :] = red.astype(BF16)
        shift = inverse * (jnp.sum(low.astype(F32) * red, axis=1, keepdims=True) / width)
        for c in columns:
            back = jnp.dot(low, down_ref[:, c], preferred_element_type=F32) * gain_ref[:, c]
            grad = g_ref[rows, c].astype(F32) + inverse * (back - x_ref[rows, c].astype(F32) * shift)
            grad_ref[rows, c] = grad.astype(BF16)

        @pl.when(sends)
        def _():
            if b == 0:
                pl.semaphore_wait(barrier, 1)
            pass_copy(b).start()
            if b == 0:
                pl.semaphore_signal(here_sem, inc=1, device_id=(before, me), device_id_type=MESH)

    work(0)

    @pl.when(jnp.logical_not(receives))
    def _():
        zero_ref[...] = jnp.zeros_like(zero_ref)
        for b, r in enumerate(blocks):
            pltpu.make_async_copy(
                zero_ref.at[pl.ds(0, BLOCK_ROWS[b])], passed_ref.at[0, r], zero_sem.at[b]
            ).start()

    for b in range(1, len(blocks)):
        work(b)

    @pl.when(section == 0)
    def _():
        pl.semaphore_wait(barrier, n - 1)

        @pl.when(receives)
        def _():
            pl.semaphore_wait(here_sem, 1)
            to_peers(round_sem)

    if pad != q:
        flat_ref[...] = jnp.zeros_like(flat_ref)
        stride = (tiles // q) * pad
    else:
        stride = tiles
    for c in range(0, width, CHUNK):
        down_term = contract_first(low_ref[...], normed_ref[:, c : c + CHUNK]) / tokens
        up_term = adapter_scale * contract_first(red_ref[...], g_ref[:, c : c + CHUNK]) / tokens
        for t, term in enumerate((down_term, up_term)):
            for inner in range(CHUNK // LANES):
                tile = c // LANES + inner
                place = tile if pad == q else (tile // q) * pad + tile % q
                flat_ref[pl.ds(t * half * pad + place, rank, stride=stride), :] = (
                    term[:, inner * LANES : (inner + 1) * LANES]
                )

    def pack(d, carry):
        vsend[d] = flat_ref[pl.ds(pl.multiple_of(d * pad, 8), pad), :].astype(BF16)
        return carry

    lax.fori_loop(0, n, pack, 0)

    @pl.when(sends)
    def _():
        pl.semaphore_wait(ready_sem, 1)

        @pl.when(receives)
        def _():
            pl.semaphore_wait(here_sem, 1)
            to_peers(round_sem)

    @pl.when(receives)
    def _():
        pl.semaphore_wait(round_sem, n - 1)
        pl.semaphore_signal(ready_sem, inc=1, device_id=(section + 1, me), device_id_type=MESH)

    def v_copy(k):
        to = lax.rem(me + k, n)
        return pltpu.make_async_remote_copy(
            src_ref=vsend.at[to],
            dst_ref=vrecv.at[me],
            send_sem=v_send_sem.at[k],
            recv_sem=v_recv_sem.at[k],
            device_id=(section, to),
            device_id_type=MESH,
        )

    def v_arrival(k):
        source = lax.rem(me + n - k, n)
        return pltpu.make_async_remote_copy(
            src_ref=vsend.at[source],
            dst_ref=vrecv.at[source],
            send_sem=v_send_sem.at[k],
            recv_sem=v_recv_sem.at[k],
            device_id=(section, source),
            device_id_type=MESH,
        )

    def v_start(k, carry):
        v_copy(k).start()
        return carry

    lax.fori_loop(1, n, v_start, 0)
    vwide[me] = vsend[me].astype(F32)

    def v_wait(k, carry):
        v_arrival(k).wait_recv()
        source = lax.rem(me + n - k, n)
        vwide[source] = vrecv[source].astype(F32)
        return carry

    lax.fori_loop(1, n, v_wait, 0)

    lane = lax.broadcasted_iota(jnp.int32, (n, LANES), 1)

    def gram_column(i, gram):
        products = jnp.sum(vwide[...] * vwide[i][None], axis=1)
        return jnp.where(lane == i, jnp.sum(products, axis=1, keepdims=True), gram)

    gram_send[...] = lax.fori_loop(0, n, gram_column, jnp.zeros((n, LANES), F32))

    base = (me // half) * half
    place = me - base

    def gram_copy(k):
        to = lax.rem(place + k, half)
        return pltpu.make_async_remote_copy(
            src_ref=gram_send,
            dst_ref=gram_recv.at[place],
            send_sem=gram_send_sem.at[k],
            recv_sem=gram_recv_sem.at[k],
            device_id=(section, base + to),
            device_id_type=MESH,
        )

    def gram_arrival(k):
        source = lax.rem(place + half - k, half)
        return pltpu.make_async_remote_copy(
            src_ref=gram_send,
            dst_ref=gram_recv.at[source],
            send_sem=gram_send_sem.at[k],
            recv_sem=gram_recv_sem.at[k],
            device_id=(section, base + source),
            device_id_type=MESH,
        )

    def gram_start(k, carry):
        gram_copy(k).start()
        return carry

    lax.fori_loop(1, half, gram_start, 0)
    gram_recv[place] = gram_send[...]

    def gram_wait(k, carry):
        gram_arrival(k).wait_recv()
        return carry

    lax.fori_loop(1, half, gram_wait, 0)

    coef = tree_coefficients(jnp.sum(gram_recv[...], axis=0), n)
    coef_ref[...] = jnp.broadcast_to(coef, (n, LANES))

    def weigh(i, total):
        return total + coef_ref[pl.ds(i, 1), :] * vwide[i]

    total = lax.fori_loop(0, n, weigh, jnp.zeros((pad, LANES), F32))
    for tile in range(q):
        pair_ref[:, tile * LANES : (tile + 1) * LANES] = total[tile : tile + 1, :].astype(BF16)

    def sent(k, carry):
        v_copy(k).wait_send()
        return carry

    lax.fori_loop(1, n, sent, 0)

    def gram_sent(k, carry):
        gram_copy(k).wait_send()
        return carry

    lax.fori_loop(1, half, gram_sent, 0)

    @pl.when(jnp.logical_not(receives))
    def _():
        for b, r in enumerate(blocks):
            pltpu.make_async_copy(
                zero_ref.at[pl.ds(0, BLOCK_ROWS[b])], passed_ref.at[0, r], zero_sem.at[b]
            ).wait()

    @pl.when(sends)
    def _():
        for b in range(len(blocks)):
            pass_copy(b).wait_send()

    @pl.when(receives)
    def _():
        for b in range(len(blocks)):
            pass_copy(b).wait_recv()


def store_results(passed_in, pair_in, passed_out, pair_out, sem):
    rows = passed_in.shape[1] // PIECES
    copies = [pltpu.make_async_copy(pair_in, pair_out, sem.at[PIECES])]
    for i in range(PIECES):
        piece = pl.ds(i * rows, rows)
        copies.append(pltpu.make_async_copy(passed_in.at[0, piece], passed_out.at[0, piece], sem.at[i]))
    for copy in copies:
        copy.start()
    for copy in copies:
        copy.wait()


def per_device(sections, n, activations, upstream, gain, down, up):
    _, tokens, width = activations.shape
    rank = down.shape[1]
    share = 2 * rank * width // n
    q = share // LANES
    pad = q if share >= width else -(-q // 16) * 16
    count = len(BLOCK_ROWS)
    anywhere = pl.BlockSpec(memory_space=pl.ANY)
    shapes = (
        jax.ShapeDtypeStruct(activations.shape, BF16),
        jax.ShapeDtypeStruct((1, share), BF16),
    )
    held = pl.pallas_call(
        functools.partial(kernel, sections, n, q, pad),
        out_shape=shapes,
        in_specs=[pl.BlockSpec(memory_space=pltpu.HBM)] * 5,
        out_specs=(anywhere, pl.BlockSpec(memory_space=pltpu.VMEM)),
        scratch_shapes=[
            pltpu.VMEM((tokens, width), BF16),
            pltpu.VMEM((tokens, width), BF16),
            pltpu.VMEM((1, width), F32),
            pltpu.VMEM((rank, width), BF16),
            pltpu.VMEM((rank, width), BF16),
            pltpu.VMEM((tokens, width), BF16),
            pltpu.VMEM((tokens, width), BF16),
            pltpu.VMEM((max(BLOCK_ROWS), width), BF16),
            pltpu.VMEM((tokens, rank), BF16),
            pltpu.VMEM((tokens, rank), BF16),
            pltpu.VMEM((n * pad, LANES), F32),
            pltpu.VMEM((n, pad, LANES), BF16),
            pltpu.VMEM((n, pad, LANES), BF16),
            pltpu.VMEM((n, pad, LANES), F32),
            pltpu.VMEM((n, LANES), F32),
            pltpu.VMEM((n // 2, n, LANES), F32),
            pltpu.VMEM((n, LANES), F32),
            pltpu.SemaphoreType.DMA((3,)),
            pltpu.SemaphoreType.DMA((count,)),
            pltpu.SemaphoreType.DMA((count,)),
            pltpu.SemaphoreType.DMA((count,)),
            pltpu.SemaphoreType.DMA((count,)),
            pltpu.SemaphoreType.DMA((count,)),
            pltpu.SemaphoreType.DMA((n,)),
            pltpu.SemaphoreType.DMA((n,)),
            pltpu.SemaphoreType.DMA((n,)),
            pltpu.SemaphoreType.DMA((n,)),
            pltpu.SemaphoreType.REGULAR,
            pltpu.SemaphoreType.REGULAR,
            pltpu.SemaphoreType.REGULAR,
        ],
        compiler_params=pltpu.CompilerParams(
            collective_id=0, has_side_effects=True, vmem_limit_bytes=40 * 2**20
        ),
        cost_estimate=pl.CostEstimate(
            flops=12 * tokens * width * rank, bytes_accessed=6 * tokens * width, transcendentals=0
        ),
    )(*[pltpu.with_memory_space_constraint(a, pltpu.HBM) for a in (activations, upstream, gain, down, up)])
    return pl.pallas_call(
        store_results,
        out_shape=shapes,
        in_specs=[anywhere, anywhere],
        out_specs=(anywhere, anywhere),
        scratch_shapes=[pltpu.SemaphoreType.DMA((PIECES + 1,))],
    )(*[pltpu.with_memory_space_constraint(value, pltpu.VMEM) for value in held])


def solution(mesh):
    return jax.shard_map(
        functools.partial(per_device, mesh.shape["section"], mesh.shape["dp"]),
        mesh=mesh,
        in_specs=(
            P("section", "dp", None),
            P("section", "dp", None),
            P("section", None),
            P("section", None, None),
            P("section", None, None),
        ),
        out_specs=(P("section", "dp", None), P("section", "dp")),
        check_vma=False,
    )
```
